32 devices in a mesh: frame: 4 (over z), patch: 8 (over y, x, core).
Axes of the slice: x: 2, y: 2, z: 4, core: 2. Of those that a mesh axis runs over, the one named last changes fastest.
Arguments:
- latent: bfloat16 [8192, 1536], P(('frame', 'patch')), parts along dimension 0, may hold values from -6 to 6
- conv_weight: float32 [9, 1536], replicated, may hold values from -4 to 4
- time_table: bfloat16 [50, 4608], replicated
- action_table: bfloat16 [18, 4608], replicated
- timestep: int32 [4], P('frame'), parts along dimension 0, may hold values from 0 to 49
- action: int32 [4], P('frame'), parts along dimension 0, may hold values from 0 to 17
- w_qkv: bfloat16 [1536, 4608], replicated, may hold values from -0.21875 to 0.21875
- w_out: bfloat16 [1536, 1536], replicated, may hold values from -0.15625 to 0.15625
- stale_kv: bfloat16 [8192, 3072], P(('frame', 'patch')), parts along dimension 0
Outputs:
- layer_out: bfloat16 [8192, 1536], P(('frame', 'patch')), parts along dimension 0
- fresh_kv: bfloat16 [8192, 3072], P(('frame', 'patch')), parts along dimension 0
The draws below stay inside these ranges and needn't reach their ends.
There are 4 independent parts, one for each index of `frame`. The reference program is written for one: setup_inputs(seed, part) draws one part's arguments, and reference() takes and returns one part's arrays. A program takes and returns all parts, laid end to end along the dimension named above; an argument that names none is the same for every part. Nothing has to cross between parts.
All inputs are finite; a program needn't handle non-finite values.
Results may differ from the reference program's by a relative error of at most 0.012.
Values may be sent and summed in bfloat16 or wider, within the bound.
A program may use at most 128 MiB of HBM per device.

```python
import jax
import jax.numpy as jnp
from jax import lax

HEADS = 24
HD = 64
D = 1536
GRID_W = 64
STEPS = 50
ACTIONS = 18
TOK_DEV = 256
TOKENS = 2048
N_PATCH = 8


def module_rows(key, count):
    base = jnp.clip(jax.random.normal(key, (count, 3 * D), jnp.float32), -6.0, 6.0)
    column = jnp.arange(3 * D, dtype=jnp.int32)[None, :]
    factor = jnp.where(column < D, 0.15, jnp.where(column < 2 * D, 0.25, 0.6))
    return (base * factor).astype(jnp.bfloat16)


def draw_time_table(key, part):
    key = jax.random.fold_in(key, 11)
    return module_rows(key, STEPS)


def draw_action_table(key, part):
    key = jax.random.fold_in(key, 13)
    return module_rows(key, ACTIONS)


def draw_stale_kv(key, part):
    key = jax.random.fold_in(key, 7)
    first = jax.random.fold_in(key, 0)
    column = jnp.arange(2 * D, dtype=jnp.int32)[None, :]
    base = jnp.clip(jax.random.normal(first, (TOKENS, 2 * D), jnp.float32), -5.0, 5.0)
    base = base * jnp.where(column < D, 1.5, 2.2)
    return base.astype(jnp.bfloat16)


def level_of(own_key, extent, shards, low, high):
    gain = 1.0
    for position, parts in shards:
        heights = jax.random.uniform(jax.random.fold_in(jax.random.fold_in(own_key, 6), position), (parts,), jnp.float32, low / len(shards), high / len(shards))
        gain = gain * jnp.repeat(jnp.exp(heights), extent[position] // parts).reshape((-1,) + (1,) * (len(extent) - 1 - position))
    return gain


def bell_draw(rng, dims, spread, limit, pieces=(), kind=jnp.bfloat16):
    values = jax.random.normal(rng, dims, jnp.float32) * spread
    if len(pieces) > 0:
        values = level_of(rng, dims, pieces, -0.22, 0.18) * values
    return jnp.clip(values, min=-limit, max=limit).astype(kind)


def setup_inputs(seed: int = 0, part: int = 0) -> dict:
    seeds = jax.random.split(jax.random.key(seed), 10)
    part_splits = jax.random.split(jax.random.fold_in(seeds[9], part), 10)
    latent = bell_draw(part_splits[0], (TOKENS, D), 1.0, 6.0, ((0, 8),))
    conv_weight = bell_draw(seeds[1], (9, D), 0.3, 4.0, (), jnp.float32)
    time_table = draw_time_table(jax.random.fold_in(seeds[9], 71), part)
    action_table = draw_action_table(jax.random.fold_in(seeds[9], 71), part)
    timestep = jax.random.randint(part_splits[4], (1,), 0, STEPS).astype(jnp.int32)
    action = jax.random.randint(part_splits[5], (1,), 0, ACTIONS).astype(jnp.int32)
    w_qkv = bell_draw(seeds[6], (D, 3 * D), (D // 2) ** -0.5, 0.21875)
    w_out = bell_draw(seeds[7], (D, D), D ** -0.5, 0.15625)
    stale_kv = draw_stale_kv(jax.random.fold_in(jax.random.fold_in(seeds[9], part), 71), part)
    return dict(latent=latent, conv_weight=conv_weight, time_table=time_table, action_table=action_table, timestep=timestep, action=action, w_qkv=w_qkv, w_out=w_out, stale_kv=stale_kv)


def lookup(table, index):
    hot = (jnp.arange(table.shape[0], dtype=jnp.int32)[None, :] == index[:, None]).astype(table.dtype)
    return jnp.dot(hot, table, preferred_element_type=jnp.float32)[0]

def reference(latent, conv_weight, time_table, action_table, timestep, action, w_qkv, w_out, stale_kv):
    grid = latent.astype(jnp.float32).reshape(-1, GRID_W, D)
    nrows = grid.shape[0]
    padded = jnp.pad(grid, ((1, 1), (1, 1), (0, 0)))
    mixed = grid
    for a in range(3):
        for b in range(3):
            mixed = mixed + padded[a:a + nrows, b:b + GRID_W] * conv_weight[3 * a + b]
    mixed = mixed.reshape(-1, D)
    modulation = lookup(time_table, timestep) + lookup(action_table, action)
    shift, scale, gate = (modulation[:D], modulation[D:2 * D], modulation[2 * D:])
    mean = lax.optimization_barrier(jnp.mean(mixed, axis=1, keepdims=True))
    var = lax.optimization_barrier(jnp.mean((mixed - mean) ** 2, axis=1, keepdims=True))
    normed = ((mixed - mean) * lax.rsqrt(var + 1e-06) * (1.0 + scale) + shift).astype(jnp.bfloat16)
    projected = jnp.dot(normed, w_qkv, preferred_element_type=jnp.float32)
    queries = projected[:, :D].astype(jnp.bfloat16)
    fresh_kv = projected[:, D:].astype(jnp.bfloat16)

    def block_out(blk):
        first = (blk * TOK_DEV).astype(jnp.int32)
        query = lax.dynamic_slice_in_dim(queries, first, TOK_DEV, 0).reshape(TOK_DEV, HEADS, HD).astype(jnp.float32)
        own = lax.dynamic_slice_in_dim(fresh_kv, first, TOK_DEV, 0)
        whole = lax.dynamic_update_slice_in_dim(stale_kv, own, first, 0)
        keys = whole[:, :D].reshape(-1, HEADS, HD).astype(jnp.float32)
        values = whole[:, D:].reshape(-1, HEADS, HD).astype(jnp.float32)
        scores = jnp.einsum('qhe,khe->hqk', query, keys) * HD ** (-0.5)
        top = lax.optimization_barrier(jnp.max(scores, axis=2, keepdims=True))
        expo = jnp.exp(scores - top)
        total = lax.optimization_barrier(jnp.sum(expo, axis=2))
        weights = lax.optimization_barrier(expo.astype(jnp.bfloat16))
        summed = jnp.einsum('hqk,khe->hqe', weights.astype(jnp.float32), values)
        result = summed / total[:, :, None]
        return jnp.transpose(result, (1, 0, 2)).reshape(TOK_DEV, D).astype(jnp.bfloat16)
    attended = lax.map(block_out, jnp.arange(N_PATCH, dtype=jnp.int32)).reshape(-1, D)
    proj = jnp.dot(attended, w_out, preferred_element_type=jnp.float32)
    layer_out = (mixed + gate * proj).astype(jnp.bfloat16)
    return (layer_out, fresh_kv)
```

```python
import functools

import jax
import jax.numpy as jnp
from jax import lax
from jax.experimental import pallas as pl
from jax.experimental.pallas import tpu as pltpu
from jax.sharding import PartitionSpec as P

HEADS = 24
GRID_W = 64
LANES = 128
GROUP = 2
CHUNK = 512


def kernel(
    count,
    timestep,
    action,
    latent,
    conv_weight,
    time_table,
    action_table,
    w_qkv,
    w_out,
    stale,
    layer_out,
    fresh,
    kv,
    wq,
    wo,
    halo,
    mixed,
    normed,
    qbd,
    acc,
    tops,
    totals,
    modulation,
    halo_send,
    halo_recv,
    own_send,
    relay_send,
    cross_send,
    recv,
    load_sem,
):
    rows, width = latent.shape
    half = rows // 2
    size = width // HEADS
    pairs = width // LANES
    chips = count // 2
    me = lax.axis_index("patch")
    core = me % 2
    chip = me // 2
    sibling = chip * 2 + (1 - core)

    def part(h):
        return pl.ds(h * half, half)

    def target(j):
        if chips == 4:
            other = chip + 1 - 2 * (chip % 2) if j == 1 else (chip + 2) % 4
        else:
            other = (chip + chips - j) % chips
        return other * 2 + core

    def send(src, role, h, sem, device):
        copy = pltpu.make_async_remote_copy(
            src_ref=src,
            dst_ref=kv.at[role - 1, part(h)],
            send_sem=sem,
            recv_sem=recv.at[role - 1, h],
            device_id={"patch": device},
            device_id_type=pl.DeviceIdType.MESH,
        )
        copy.start()
        return copy

    def arrived(role, h):
        pltpu.make_async_remote_copy(
            src_ref=kv.at[role - 1, part(h)],
            dst_ref=kv.at[role - 1, part(h)],
            send_sem=cross_send.at[0],
            recv_sem=recv.at[role - 1, h],
            device_id={"patch": sibling},
            device_id_type=pl.DeviceIdType.MESH,
        ).wait_recv()

    loads = [
        pltpu.make_async_copy(w_qkv, wq, load_sem.at[0]),
        pltpu.make_async_copy(w_out, wo, load_sem.at[1]),
    ]
    for load in loads:
        load.start()

    barrier = pltpu.get_barrier_semaphore()
    for step in range(1, count):
        pl.semaphore_signal(
            barrier,
            inc=1,
            device_id={"patch": (me + step) % count},
            device_id_type=pl.DeviceIdType.MESH,
        )
    pl.semaphore_wait(barrier, count - 1)

    edges = []
    for slot, (start, device) in enumerate(
        ((rows - GRID_W, (me + 1) % count), (0, (me + count - 1) % count))
    ):
        copy = pltpu.make_async_remote_copy(
            src_ref=latent.at[pl.ds(start, GRID_W)],
            dst_ref=halo.at[slot],
            send_sem=halo_send.at[slot],
            recv_sem=halo_recv.at[slot],
            device_id={"patch": device},
            device_id_type=pl.DeviceIdType.MESH,
        )
        copy.start()
        edges.append(copy)

    sent = []
    direct = (1, 2) if chips == 4 else tuple(range(1, chips))
    for order in range(2):
        for j in direct:
            h = order if j % 2 == 1 else 1 - order
            sent.append(send(stale.at[part(h)], 2 * j, h, own_send.at[j, h], target(j)))
        sent.append(send(stale.at[part(order)], 1, order, own_send.at[0, order], sibling))

    def relay(j, h):
        arrived(2 * j, h)
        if chips == 4 and (j, h) == (1, 0):
            sent.append(send(kv.at[1, part(0)], 6, 0, cross_send.at[0], target(2)))
        if chips == 4 and (j, h) == (2, 1):
            sent.append(send(kv.at[3, part(1)], 6, 1, cross_send.at[1], target(1)))
        sent.append(
            send(kv.at[2 * j - 1, part(h)], 2 * j + 1, h, relay_send.at[j - 1, h], sibling)
        )

    def pick(table, index):
        hot = lax.broadcasted_iota(jnp.int32, table.shape, 0) == index
        return jnp.sum(
            jnp.where(hot, table[...].astype(jnp.float32), 0.0), axis=0, keepdims=True
        )

    modulation[...] = pick(time_table, timestep[0]) + pick(action_table, action[0])

    nrows = rows // GRID_W

    def stem(r):
        def body(c, carry):
            cols = pl.ds(pl.multiple_of(c * 2 * LANES, 2 * LANES), 2 * LANES)
            taps = conv_weight[:, cols]
            lines = []
            for a in (r - 1, r, r + 1):
                if a < 0:
                    line = jnp.where(me > 0, halo[0, :, cols].astype(jnp.float32), 0.0)
                elif a >= nrows:
                    line = jnp.where(me < count - 1, halo[1, :, cols].astype(jnp.float32), 0.0)
                else:
                    line = latent[pl.ds(a * GRID_W, GRID_W), cols].astype(jnp.float32)
                lines.append(line)
            sums = []
            for b in range(3):
                total = lines[0] * taps[b : b + 1]
                total = total + lines[1] * taps[3 + b : 4 + b]
                sums.append(total + lines[2] * taps[6 + b : 7 + b])
            place = lax.broadcasted_iota(jnp.int32, sums[0].shape, 0)
            before = jnp.where(place == 0, 0.0, pltpu.roll(sums[0], 1, 0))
            after = jnp.where(place == GRID_W - 1, 0.0, pltpu.roll(sums[2], GRID_W - 1, 0))
            mixed[pl.ds(r * GRID_W, GRID_W), cols] = lines[1] + sums[1] + (before + after)
            return carry

        lax.fori_loop(0, width // (2 * LANES), body, 0)

    for r in range(1, nrows - 1):
        stem(r)
    for edge in edges:
        edge.wait_recv()
    stem(0)
    stem(nrows - 1)

    def norm(r, carry):
        span = pl.ds(pl.multiple_of(r * 32, 32), 32)
        x = mixed[span, :]
        mean = jnp.mean(x, axis=1, keepdims=True)
        centred = x - mean
        var = jnp.mean(centred * centred, axis=1, keepdims=True)
        gain = 1.0 + modulation[:, width : 2 * width]
        normed[span, :] = (
            centred * lax.rsqrt(var + 1e-06) * gain + modulation[:, :width]
        ).astype(jnp.bfloat16)
        return carry

    lax.fori_loop(0, rows // 32, norm, 0)

    loads[0].wait()
    qbd[...] = jnp.zeros_like(qbd)
    per = CHUNK // LANES

    def project(c):
        cols = pl.ds(pl.multiple_of(c * CHUNK, CHUNK), CHUNK)
        return jnp.dot(normed[...], wq[:, cols], preferred_element_type=jnp.float32)

    def queries(c, carry):
        block = project(c) * size ** (-0.5)
        for u in range(per):
            flipped = jnp.transpose(block[:, u * LANES : (u + 1) * LANES]).astype(jnp.bfloat16)
            qbd[c * per + u, :size, :rows] = flipped[:size]
            qbd[c * per + u, size:, rows:] = flipped[size:]
        return carry

    lax.fori_loop(0, width // CHUNK, queries, 0)

    def keys_values(c, carry):
        cols = pl.ds(pl.multiple_of(c * CHUNK, CHUNK), CHUNK)
        fresh[:, cols] = project(c + width // CHUNK).astype(jnp.bfloat16)
        return carry

    lax.fori_loop(0, 2 * width // CHUNK, keys_values, 0)

    def attend(read, first=False):
        def body(g, carry):
            done = []
            for u in range(GROUP):
                i = g * GROUP + u
                col = pl.multiple_of(i * LANES, LANES)
                scores = jnp.dot(
                    read(pl.ds(col, LANES)), qbd[i], preferred_element_type=jnp.float32
                )
                top = jnp.max(scores, axis=0, keepdims=True)
                if not first:
                    top = jnp.maximum(top, tops[i])
                expo = jnp.exp(scores - top)
                total = jnp.sum(expo, axis=0, keepdims=True)
                weights = expo.astype(jnp.bfloat16)
                flipped = jnp.transpose(read(pl.ds(pl.multiple_of(width + col, LANES), LANES)))
                summed = jnp.concatenate(
                    [
                        jnp.dot(
                            flipped[:size], weights[:, :rows], preferred_element_type=jnp.float32
                        ),
                        jnp.dot(
                            flipped[size:], weights[:, rows:], preferred_element_type=jnp.float32
                        ),
                    ],
                    axis=1,
                )
                if not first:
                    factor = jnp.exp(tops[i] - top)
                    total = total + totals[i] * factor
                    summed = summed + acc[i] * factor
                done.append((i, top, total, summed))
            for i, top, total, summed in done:
                tops[i] = top
                totals[i] = total
                acc[i] = summed
            return carry

        lax.fori_loop(0, pairs // GROUP, body, 0)

    def two(first, second):
        def read(cols):
            return jnp.concatenate(
                [kv[role - 1, part(h), cols] for role, h in (first, second)], axis=0
            )

        return read

    attend(lambda cols: fresh[:, cols], first=True)
    arrived(1, 0)
    arrived(1, 1)
    attend(two((1, 0), (1, 1)))
    if chips == 4:
        plan = [((1, 0), (2, 1)), ((1, 1), (2, 0)), ((3, 0), (3, 1))]
    else:
        plan = [((j, 0), (j, 1)) for j in range(1, chips)]
    for one, other in plan:
        relay(*one)
        relay(*other)
        attend(two((2 * one[0], one[1]), (2 * other[0], other[1])))
        arrived(2 * one[0] + 1, one[1])
        arrived(2 * other[0] + 1, other[1])
        attend(two((2 * one[0] + 1, one[1]), (2 * other[0] + 1, other[1])))

    def finish(i, carry):
        result = acc[i] / totals[i]
        stacked = jnp.concatenate([result[:, :rows], result[:, rows:]], axis=0)
        cols = pl.ds(pl.multiple_of(i * LANES, LANES), LANES)
        normed[:, cols] = jnp.transpose(stacked).astype(jnp.bfloat16)
        return carry

    lax.fori_loop(0, pairs, finish, 0)
    loads[1].wait()

    def output(c, carry):
        cols = pl.ds(pl.multiple_of(c * CHUNK, CHUNK), CHUNK)
        proj = jnp.dot(normed[...], wo[:, cols], preferred_element_type=jnp.float32)
        gate = modulation[:, pl.ds(pl.multiple_of(2 * width + c * CHUNK, CHUNK), CHUNK)]
        layer_out[:, cols] = (mixed[:, cols] + gate * proj).astype(jnp.bfloat16)
        return carry

    lax.fori_loop(0, width // CHUNK, output, 0)

    for copy in edges + sent:
        copy.wait_send()


def per_device(
    count, latent, conv_weight, time_table, action_table, timestep, action, w_qkv, w_out, stale_kv
):
    rows, width = latent.shape
    pairs = width // LANES
    size = width // HEADS
    chips = count // 2
    vmem = pl.BlockSpec(memory_space=pltpu.VMEM)
    smem = pl.BlockSpec(memory_space=pltpu.SMEM)
    anywhere = pl.BlockSpec(memory_space=pl.ANY)
    dma = pltpu.SemaphoreType.DMA
    return pl.pallas_call(
        functools.partial(kernel, count),
        out_shape=(
            jax.ShapeDtypeStruct((rows, width), jnp.bfloat16),
            jax.ShapeDtypeStruct((rows, 2 * width), jnp.bfloat16),
        ),
        in_specs=[smem, smem, vmem, vmem, vmem, vmem, anywhere, anywhere, anywhere],
        out_specs=(vmem, vmem),
        scratch_shapes=[
            pltpu.VMEM((count - 1, rows, 2 * width), jnp.bfloat16),
            pltpu.VMEM(w_qkv.shape, jnp.bfloat16),
            pltpu.VMEM(w_out.shape, jnp.bfloat16),
            pltpu.VMEM((2, GRID_W, width), jnp.bfloat16),
            pltpu.VMEM((rows, width), jnp.float32),
            pltpu.VMEM((rows, width), jnp.bfloat16),
            pltpu.VMEM((pairs, LANES, 2 * rows), jnp.bfloat16),
            pltpu.VMEM((pairs, size, 2 * rows), jnp.float32),
            pltpu.VMEM((pairs, 1, 2 * rows), jnp.float32),
            pltpu.VMEM((pairs, 1, 2 * rows), jnp.float32),
            pltpu.VMEM((1, 3 * width), jnp.float32),
            dma((2,)),
            dma((2,)),
            dma((chips, 2)),
            dma((chips - 1, 2)),
            dma((2,)),
            dma((count - 1, 2)),
            dma((2,)),
        ],
        compiler_params=pltpu.CompilerParams(
            collective_id=0, has_side_effects=True, vmem_limit_bytes=60 * 2**20
        ),
        cost_estimate=pl.CostEstimate(
            flops=8 * 10**9, bytes_accessed=30 * 2**20, transcendentals=13 * 10**6
        ),
    )(timestep, action, latent, conv_weight, time_table, action_table, w_qkv, w_out, stale_kv)


def solution(mesh):
    in_specs = (
        P(("frame", "patch"), None),
        P(),
        P(),
        P(),
        P("frame"),
        P("frame"),
        P(),
        P(),
        P(("frame", "patch"), None),
    )
    out_specs = (P(("frame", "patch"), None), P(("frame", "patch"), None))
    return jax.shard_map(
        functools.partial(per_device, mesh.shape["patch"]),
        mesh=mesh,
        in_specs=in_specs,
        out_specs=out_specs,
        check_vma=False,
    )
```

```python
import functools

import jax
import jax.numpy as jnp
from jax import lax
from jax.experimental import pallas as pl
from jax.experimental.pallas import tpu as pltpu
from jax.sharding import PartitionSpec as P

HEADS = 24
GRID_W = 64
LANES = 128
GROUP = 2
CHUNK = 512


def kernel(
    count,
    timestep,
    action,
    latent,
    conv_weight,
    time_table,
    action_table,
    w_qkv,
    w_out,
    stale,
    layer_out,
    fresh,
    kv,
    wq,
    wo,
    halo,
    mixed,
    normed,
    qbd,
    acc,
    tops,
    totals,
    modulation,
    halo_send,
    halo_recv,
    own_send,
    relay_send,
    cross_send,
    recv,
    load_sem,
):
    rows, width = latent.shape
    half = rows // 2
    size = width // HEADS
    pairs = width // LANES
    chips = count // 2
    me = lax.axis_index("patch")
    core = me % 2
    chip = me // 2
    sibling = chip * 2 + (1 - core)

    def part(h):
        return pl.ds(h * half, half)

    def target(j):
        if chips == 4:
            other = chip + 1 - 2 * (chip % 2) if j == 1 else (chip + 2) % 4
        else:
            other = (chip + chips - j) % chips
        return other * 2 + core

    def send(src, role, h, sem, device):
        copy = pltpu.make_async_remote_copy(
            src_ref=src,
            dst_ref=kv.at[role - 1, part(h)],
            send_sem=sem,
            recv_sem=recv.at[role - 1, h],
            device_id={"patch": device},
            device_id_type=pl.DeviceIdType.MESH,
        )
        copy.start()
        return copy

    def arrived(role, h):
        pltpu.make_async_remote_copy(
            src_ref=kv.at[role - 1, part(h)],
            dst_ref=kv.at[role - 1, part(h)],
            send_sem=cross_send.at[0],
            recv_sem=recv.at[role - 1, h],
            device_id={"patch": sibling},
            device_id_type=pl.DeviceIdType.MESH,
        ).wait_recv()

    loads = [
        pltpu.make_async_copy(w_qkv, wq, load_sem.at[0]),
        pltpu.make_async_copy(w_out, wo, load_sem.at[1]),
    ]
    for load in loads:
        load.start()

    barrier = pltpu.get_barrier_semaphore()
    for step in range(1, count):
        pl.semaphore_signal(
            barrier,
            inc=1,
            device_id={"patch": (me + step) % count},
            device_id_type=pl.DeviceIdType.MESH,
        )
    pl.semaphore_wait(barrier, count - 1)

    edges = []
    for slot, (start, device) in enumerate(
        ((rows - GRID_W, (me + 1) % count), (0, (me + count - 1) % count))
    ):
        copy = pltpu.make_async_remote_copy(
            src_ref=latent.at[pl.ds(start, GRID_W)],
            dst_ref=halo.at[slot],
            send_sem=halo_send.at[slot],
            recv_sem=halo_recv.at[slot],
            device_id={"patch": device},
            device_id_type=pl.DeviceIdType.MESH,
        )
        copy.start()
        edges.append(copy)

    sent = []
    direct = (1, 2) if chips == 4 else tuple(range(1, chips))
    for order in range(2):
        for j in direct:
            h = order if j % 2 == 1 else 1 - order
            sent.append(send(stale.at[part(h)], 2 * j, h, own_send.at[j, h], target(j)))
        sent.append(send(stale.at[part(order)], 1, order, own_send.at[0, order], sibling))

    def relay(j, h):
        arrived(2 * j, h)
        if chips == 4 and (j, h) == (1, 0):
            sent.append(send(kv.at[1, part(0)], 6, 0, cross_send.at[0], target(2)))
        if chips == 4 and (j, h) == (2, 1):
            sent.append(send(kv.at[3, part(1)], 6, 1, cross_send.at[1], target(1)))
        sent.append(
            send(kv.at[2 * j - 1, part(h)], 2 * j + 1, h, relay_send.at[j - 1, h], sibling)
        )

    def pick(table, index):
        hot = lax.broadcasted_iota(jnp.int32, table.shape, 0) == index
        return jnp.sum(
            jnp.where(hot, table[...].astype(jnp.float32), 0.0), axis=0, keepdims=True
        )

    modulation[...] = pick(time_table, timestep[0]) + pick(action_table, action[0])

    nrows = rows // GRID_W

    def stem(r):
        def body(c, carry):
            cols = pl.ds(pl.multiple_of(c * 2 * LANES, 2 * LANES), 2 * LANES)
            taps = conv_weight[:, cols]
            lines = []
            for a in (r - 1, r, r + 1):
                if a < 0:
                    line = jnp.where(me > 0, halo[0, :, cols].astype(jnp.float32), 0.0)
                elif a >= nrows:
                    line = jnp.where(me < count - 1, halo[1, :, cols].astype(jnp.float32), 0.0)
                else:
                    line = latent[pl.ds(a * GRID_W, GRID_W), cols].astype(jnp.float32)
                lines.append(line)
            sums = []
            for b in range(3):
                total = lines[0] * taps[b : b + 1]
                total = total + lines[1] * taps[3 + b : 4 + b]
                sums.append(total + lines[2] * taps[6 + b : 7 + b])
            place = lax.broadcasted_iota(jnp.int32, sums[0].shape, 0)
            before = jnp.where(place == 0, 0.0, pltpu.roll(sums[0], 1, 0))
            after = jnp.where(place == GRID_W - 1, 0.0, pltpu.roll(sums[2], GRID_W - 1, 0))
            mixed[pl.ds(r * GRID_W, GRID_W), cols] = lines[1] + sums[1] + (before + after)
            return carry

        lax.fori_loop(0, width // (2 * LANES), body, 0)

    for r in range(1, nrows - 1):
        stem(r)
    for edge in edges:
        edge.wait_recv()
    stem(0)
    stem(nrows - 1)

    def norm(r, carry):
        span = pl.ds(pl.multiple_of(r * 32, 32), 32)
        x = mixed[span, :]
        mean = jnp.mean(x, axis=1, keepdims=True)
        centred = x - mean
        var = jnp.mean(centred * centred, axis=1, keepdims=True)
        gain = 1.0 + modulation[:, width : 2 * width]
        normed[span, :] = (
            centred * lax.rsqrt(var + 1e-06) * gain + modulation[:, :width]
        ).astype(jnp.bfloat16)
        return carry

    lax.fori_loop(0, rows // 32, norm, 0)

    loads[0].wait()
    qbd[...] = jnp.zeros_like(qbd)
    per = CHUNK // LANES

    def project(c):
        cols = pl.ds(pl.multiple_of(c * CHUNK, CHUNK), CHUNK)
        return jnp.dot(normed[...], wq[:, cols], preferred_element_type=jnp.float32)

    def queries(c, carry):
        block = project(c) * size ** (-0.5)
        for u in range(per):
            flipped = jnp.transpose(block[:, u * LANES : (u + 1) * LANES]).astype(jnp.bfloat16)
            qbd[c * per + u, :size, :rows] = flipped[:size]
            qbd[c * per + u, size:, rows:] = flipped[size:]
        return carry

    lax.fori_loop(0, width // CHUNK, queries, 0)

    def keys_values(c, carry):
        cols = pl.ds(pl.multiple_of(c * CHUNK, CHUNK), CHUNK)
        fresh[:, cols] = project(c + width // CHUNK).astype(jnp.bfloat16)
        return carry

    lax.fori_loop(0, 2 * width // CHUNK, keys_values, 0)

    def attend(read, first=False):
        def body(g, carry):
            done = []
            for u in range(GROUP):
                i = g * GROUP + u
                col = pl.multiple_of(i * LANES, LANES)
                scores = jnp.dot(
                    read(pl.ds(col, LANES)), qbd[i], preferred_element_type=jnp.float32
                )
                top = jnp.max(scores, axis=0, keepdims=True)
                if not first:
                    top = jnp.maximum(top, tops[i])
                expo = jnp.exp(scores - top)
                total = jnp.sum(expo, axis=0, keepdims=True)
                weights = expo.astype(jnp.bfloat16)
                flipped = jnp.transpose(read(pl.ds(pl.multiple_of(width + col, LANES), LANES)))
                summed = jnp.concatenate(
                    [
                        jnp.dot(
                            flipped[:size], weights[:, :rows], preferred_element_type=jnp.float32
                        ),
                        jnp.dot(
                            flipped[size:], weights[:, rows:], preferred_element_type=jnp.float32
                        ),
                    ],
                    axis=1,
                )
                if not first:
                    factor = jnp.exp(tops[i] - top)
                    total = total + totals[i] * factor
                    summed = summed + acc[i] * factor
                done.append((i, top, total, summed))
            for i, top, total, summed in done:
                tops[i] = top
                totals[i] = total
                acc[i] = summed
            return carry

        lax.fori_loop(0, pairs // GROUP, body, 0)

    def landed(pieces):
        def read(cols):
            return jnp.concatenate(
                [kv[role - 1, part(h), cols] for role, h in pieces], axis=0
            )

        return read

    arrived(1, 0)
    arrived(1, 1)
    beside = landed([(1, 0), (1, 1)])
    attend(lambda cols: jnp.concatenate([fresh[:, cols], beside(cols)], axis=0), first=True)
    if chips == 4:
        plan = [((1, 0), (2, 1)), ((1, 1), (2, 0)), ((3, 0), (3, 1))]
    else:
        plan = [((j, 0), (j, 1)) for j in range(1, chips)]
    for pair in plan:
        for j, h in pair:
            relay(j, h)
        for j, h in pair:
            arrived(2 * j + 1, h)
        attend(landed([(2 * j + c, h) for j, h in pair for c in range(2)]))

    def finish(i, carry):
        result = acc[i] / totals[i]
        stacked = jnp.concatenate([result[:, :rows], result[:, rows:]], axis=0)
        cols = pl.ds(pl.multiple_of(i * LANES, LANES), LANES)
        normed[:, cols] = jnp.transpose(stacked).astype(jnp.bfloat16)
        return carry

    lax.fori_loop(0, pairs, finish, 0)
    loads[1].wait()

    def output(c, carry):
        cols = pl.ds(pl.multiple_of(c * CHUNK, CHUNK), CHUNK)
        proj = jnp.dot(normed[...], wo[:, cols], preferred_element_type=jnp.float32)
        gate = modulation[:, pl.ds(pl.multiple_of(2 * width + c * CHUNK, CHUNK), CHUNK)]
        layer_out[:, cols] = (mixed[:, cols] + gate * proj).astype(jnp.bfloat16)
        return carry

    lax.fori_loop(0, width // CHUNK, output, 0)

    for copy in edges + sent:
        copy.wait_send()


def per_device(
    count, latent, conv_weight, time_table, action_table, timestep, action, w_qkv, w_out, stale_kv
):
    rows, width = latent.shape
    pairs = width // LANES
    size = width // HEADS
    chips = count // 2
    vmem = pl.BlockSpec(memory_space=pltpu.VMEM)
    smem = pl.BlockSpec(memory_space=pltpu.SMEM)
    anywhere = pl.BlockSpec(memory_space=pl.ANY)
    dma = pltpu.SemaphoreType.DMA
    return pl.pallas_call(
        functools.partial(kernel, count),
        out_shape=(
            jax.ShapeDtypeStruct((rows, width), jnp.bfloat16),
            jax.ShapeDtypeStruct((rows, 2 * width), jnp.bfloat16),
        ),
        in_specs=[smem, smem, vmem, vmem, vmem, vmem, anywhere, anywhere, anywhere],
        out_specs=(vmem, vmem),
        scratch_shapes=[
            pltpu.VMEM((count - 1, rows, 2 * width), jnp.bfloat16),
            pltpu.VMEM(w_qkv.shape, jnp.bfloat16),
            pltpu.VMEM(w_out.shape, jnp.bfloat16),
            pltpu.VMEM((2, GRID_W, width), jnp.bfloat16),
            pltpu.VMEM((rows, width), jnp.float32),
            pltpu.VMEM((rows, width), jnp.bfloat16),
            pltpu.VMEM((pairs, LANES, 2 * rows), jnp.bfloat16),
            pltpu.VMEM((pairs, size, 2 * rows), jnp.float32),
            pltpu.VMEM((pairs, 1, 2 * rows), jnp.float32),
            pltpu.VMEM((pairs, 1, 2 * rows), jnp.float32),
            pltpu.VMEM((1, 3 * width), jnp.float32),
            dma((2,)),
            dma((2,)),
            dma((chips, 2)),
            dma((chips - 1, 2)),
            dma((2,)),
            dma((count - 1, 2)),
            dma((2,)),
        ],
        compiler_params=pltpu.CompilerParams(
            collective_id=0, has_side_effects=True, vmem_limit_bytes=60 * 2**20
        ),
        cost_estimate=pl.CostEstimate(
            flops=8 * 10**9, bytes_accessed=30 * 2**20, transcendentals=13 * 10**6
        ),
    )(timestep, action, latent, conv_weight, time_table, action_table, w_qkv, w_out, stale_kv)


def solution(mesh):
    in_specs = (
        P(("frame", "patch"), None),
        P(),
        P(),
        P(),
        P("frame"),
        P("frame"),
        P(),
        P(),
        P(("frame", "patch"), None),
    )
    out_specs = (P(("frame", "patch"), None), P(("frame", "patch"), None))
    return jax.shard_map(
        functools.partial(per_device, mesh.shape["patch"]),
        mesh=mesh,
        in_specs=in_specs,
        out_specs=out_specs,
        check_vma=False,
    )
```

```python
import functools

import jax
import jax.numpy as jnp
from jax import lax
from jax.experimental import pallas as pl
from jax.experimental.pallas import tpu as pltpu
from jax.sharding import PartitionSpec as P

HEADS = 24
GRID_W = 64
LANES = 128
GROUP = 2
CHUNK = 512


def prepare(
    count,
    timestep,
    action,
    latent,
    conv_weight,
    time_table,
    action_table,
    halo,
    edges,
    mixed,
    normed,
    modulation,
):
    rows, width = latent.shape
    me = lax.axis_index("patch")

    def pick(table, index):
        hot = lax.broadcasted_iota(jnp.int32, table.shape, 0) == index
        return jnp.sum(
            jnp.where(hot, table[...].astype(jnp.float32), 0.0), axis=0, keepdims=True
        )

    modulation[...] = pick(time_table, timestep[0]) + pick(action_table, action[0])

    nrows = rows // GRID_W

    def stem(r):
        def body(c, carry):
            cols = pl.ds(pl.multiple_of(c * 2 * LANES, 2 * LANES), 2 * LANES)
            taps = conv_weight[:, cols]
            lines = []
            for a in (r - 1, r, r + 1):
                if a < 0:
                    line = jnp.where(me > 0, halo[0, :, cols].astype(jnp.float32), 0.0)
                elif a >= nrows:
                    line = jnp.where(me < count - 1, halo[1, :, cols].astype(jnp.float32), 0.0)
                else:
                    line = latent[pl.ds(a * GRID_W, GRID_W), cols].astype(jnp.float32)
                lines.append(line)
            sums = []
            for b in range(3):
                total = lines[0] * taps[b : b + 1]
                total = total + lines[1] * taps[3 + b : 4 + b]
                sums.append(total + lines[2] * taps[6 + b : 7 + b])
            place = lax.broadcasted_iota(jnp.int32, sums[0].shape, 0)
            before = jnp.where(place == 0, 0.0, pltpu.roll(sums[0], 1, 0))
            after = jnp.where(place == GRID_W - 1, 0.0, pltpu.roll(sums[2], GRID_W - 1, 0))
            mixed[pl.ds(r * GRID_W, GRID_W), cols] = lines[1] + sums[1] + (before + after)
            return carry

        lax.fori_loop(0, width // (2 * LANES), body, 0)

    for r in range(1, nrows - 1):
        stem(r)
    for edge in edges:
        edge.wait_recv()
    stem(0)
    stem(nrows - 1)

    def norm(r, carry):
        span = pl.ds(pl.multiple_of(r * 32, 32), 32)
        x = mixed[span, :]
        mean = jnp.mean(x, axis=1, keepdims=True)
        centred = x - mean
        var = jnp.mean(centred * centred, axis=1, keepdims=True)
        gain = 1.0 + modulation[:, width : 2 * width]
        normed[span, :] = (
            centred * lax.rsqrt(var + 1e-06) * gain + modulation[:, :width]
        ).astype(jnp.bfloat16)
        return carry

    lax.fori_loop(0, rows // 32, norm, 0)


def kernel(
    count,
    timestep,
    action,
    latent,
    conv_weight,
    time_table,
    action_table,
    w_qkv,
    w_out,
    stale,
    layer_out,
    fresh,
    kv,
    wq,
    wo,
    halo,
    mixed,
    normed,
    qbd,
    acc,
    tops,
    totals,
    modulation,
    halo_send,
    halo_recv,
    own_send,
    relay_send,
    cross_send,
    recv,
    load_sem,
):
    rows, width = latent.shape
    half = rows // 2
    size = width // HEADS
    pairs = width // LANES
    chips = count // 2
    me = lax.axis_index("patch")
    core = me % 2
    chip = me // 2
    sibling = chip * 2 + (1 - core)

    def part(h):
        return pl.ds(h * half, half)

    def target(j):
        if chips == 4:
            other = chip + 1 - 2 * (chip % 2) if j == 1 else (chip + 2) % 4
        else:
            other = (chip + chips - j) % chips
        return other * 2 + core

    def send(src, role, h, sem, device):
        copy = pltpu.make_async_remote_copy(
            src_ref=src,
            dst_ref=kv.at[role - 1, part(h)],
            send_sem=sem,
            recv_sem=recv.at[role - 1, h],
            device_id={"patch": device},
            device_id_type=pl.DeviceIdType.MESH,
        )
        copy.start()
        return copy

    def arrived(role, h):
        pltpu.make_async_remote_copy(
            src_ref=kv.at[role - 1, part(h)],
            dst_ref=kv.at[role - 1, part(h)],
            send_sem=cross_send.at[0],
            recv_sem=recv.at[role - 1, h],
            device_id={"patch": sibling},
            device_id_type=pl.DeviceIdType.MESH,
        ).wait_recv()

    loads = [
        pltpu.make_async_copy(w_qkv, wq, load_sem.at[0]),
        pltpu.make_async_copy(w_out, wo, load_sem.at[1]),
    ]
    for load in loads:
        load.start()

    barrier = pltpu.get_barrier_semaphore()
    for step in range(1, count):
        pl.semaphore_signal(
            barrier,
            inc=1,
            device_id={"patch": (me + step) % count},
            device_id_type=pl.DeviceIdType.MESH,
        )
    pl.semaphore_wait(barrier, count - 1)

    edges = []
    for slot, (start, device) in enumerate(
        ((rows - GRID_W, (me + 1) % count), (0, (me + count - 1) % count))
    ):
        copy = pltpu.make_async_remote_copy(
            src_ref=latent.at[pl.ds(start, GRID_W)],
            dst_ref=halo.at[slot],
            send_sem=halo_send.at[slot],
            recv_sem=halo_recv.at[slot],
            device_id={"patch": device},
            device_id_type=pl.DeviceIdType.MESH,
        )
        copy.start()
        edges.append(copy)

    sent = []
    direct = (1, 2) if chips == 4 else tuple(range(1, chips))
    for order in range(2):
        for j in direct:
            h = order if j % 2 == 1 else 1 - order
            sent.append(send(stale.at[part(h)], 2 * j, h, own_send.at[j, h], target(j)))
        sent.append(send(stale.at[part(order)], 1, order, own_send.at[0, order], sibling))

    def relay(j, h):
        arrived(2 * j, h)
        if chips == 4 and (j, h) == (1, 0):
            sent.append(send(kv.at[1, part(0)], 6, 0, cross_send.at[0], target(2)))
        if chips == 4 and (j, h) == (2, 1):
            sent.append(send(kv.at[3, part(1)], 6, 1, cross_send.at[1], target(1)))
        sent.append(
            send(kv.at[2 * j - 1, part(h)], 2 * j + 1, h, relay_send.at[j - 1, h], sibling)
        )

    prepare(
        count, timestep, action, latent, conv_weight, time_table, action_table,
        halo, edges, mixed, normed, modulation,
    )

    loads[0].wait()
    qbd[...] = jnp.zeros_like(qbd)
    per = CHUNK // LANES

    def project(c):
        cols = pl.ds(pl.multiple_of(c * CHUNK, CHUNK), CHUNK)
        return jnp.dot(normed[...], wq[:, cols], preferred_element_type=jnp.float32)

    def queries(c, carry):
        block = project(c) * size ** (-0.5)
        for u in range(per):
            flipped = jnp.transpose(block[:, u * LANES : (u + 1) * LANES]).astype(jnp.bfloat16)
            qbd[c * per + u, :size, :rows] = flipped[:size]
            qbd[c * per + u, size:, rows:] = flipped[size:]
        return carry

    lax.fori_loop(0, width // CHUNK, queries, 0)

    def keys_values(c, carry):
        cols = pl.ds(pl.multiple_of(c * CHUNK, CHUNK), CHUNK)
        fresh[:, cols] = project(c + width // CHUNK).astype(jnp.bfloat16)
        return carry

    lax.fori_loop(0, 2 * width // CHUNK, keys_values, 0)

    def attend(read, first=False):
        def body(g, carry):
            done = []
            for u in range(GROUP):
                i = g * GROUP + u
                col = pl.multiple_of(i * LANES, LANES)
                scores = jnp.dot(
                    read(pl.ds(col, LANES)), qbd[i], preferred_element_type=jnp.float32
                )
                top = jnp.max(scores, axis=0, keepdims=True)
                if not first:
                    top = jnp.maximum(top, tops[i])
                expo = jnp.exp(scores - top)
                total = jnp.sum(expo, axis=0, keepdims=True)
                weights = expo.astype(jnp.bfloat16)
                flipped = jnp.transpose(read(pl.ds(pl.multiple_of(width + col, LANES), LANES)))
                summed = jnp.concatenate(
                    [
                        jnp.dot(
                            flipped[:size], weights[:, :rows], preferred_element_type=jnp.float32
                        ),
                        jnp.dot(
                            flipped[size:], weights[:, rows:], preferred_element_type=jnp.float32
                        ),
                    ],
                    axis=1,
                )
                if not first:
                    factor = jnp.exp(tops[i] - top)
                    total = total + totals[i] * factor
                    summed = summed + acc[i] * factor
                done.append((i, top, total, summed))
            for i, top, total, summed in done:
                tops[i] = top
                totals[i] = total
                acc[i] = summed
            return carry

        lax.fori_loop(0, pairs // GROUP, body, 0)

    def landed(pieces):
        def read(cols):
            return jnp.concatenate(
                [kv[role - 1, part(h), cols] for role, h in pieces], axis=0
            )

        return read

    arrived(1, 0)
    arrived(1, 1)
    beside = landed([(1, 0), (1, 1)])
    attend(lambda cols: jnp.concatenate([fresh[:, cols], beside(cols)], axis=0), first=True)
    if chips == 4:
        plan = [((1, 0), (2, 1)), ((1, 1), (2, 0)), ((3, 0), (3, 1))]
    else:
        plan = [((j, 0), (j, 1)) for j in range(1, chips)]
    for pair in plan:
        for j, h in pair:
            relay(j, h)
        for j, h in pair:
            arrived(2 * j + 1, h)
        attend(landed([(2 * j + c, h) for j, h in pair for c in range(2)]))

    def finish(i, carry):
        result = acc[i] / totals[i]
        stacked = jnp.concatenate([result[:, :rows], result[:, rows:]], axis=0)
        cols = pl.ds(pl.multiple_of(i * LANES, LANES), LANES)
        normed[:, cols] = jnp.transpose(stacked).astype(jnp.bfloat16)
        return carry

    lax.fori_loop(0, pairs, finish, 0)
    loads[1].wait()

    def output(c, carry):
        cols = pl.ds(pl.multiple_of(c * CHUNK, CHUNK), CHUNK)
        proj = jnp.dot(normed[...], wo[:, cols], preferred_element_type=jnp.float32)
        gate = modulation[:, pl.ds(pl.multiple_of(2 * width + c * CHUNK, CHUNK), CHUNK)]
        layer_out[:, cols] = (mixed[:, cols] + gate * proj).astype(jnp.bfloat16)
        return carry

    lax.fori_loop(0, width // CHUNK, output, 0)

    for copy in edges + sent:
        copy.wait_send()


def remote(src, dst, send_sem, recv_sem, device):
    return pltpu.make_async_remote_copy(
        src_ref=src,
        dst_ref=dst,
        send_sem=send_sem,
        recv_sem=recv_sem,
        device_id={"patch": device},
        device_id_type=pl.DeviceIdType.MESH,
    )


def fold(state, keys, values, query, size, rows):
    scores = jnp.dot(keys, query, preferred_element_type=jnp.float32)
    top = jnp.max(scores, axis=0, keepdims=True)
    if state is not None:
        top = jnp.maximum(top, state[0])
    expo = jnp.exp(scores - top)
    total = jnp.sum(expo, axis=0, keepdims=True)
    weights = expo.astype(jnp.bfloat16)
    flipped = jnp.transpose(values)
    summed = jnp.concatenate(
        [
            jnp.dot(flipped[:size], weights[:, :rows], preferred_element_type=jnp.float32),
            jnp.dot(flipped[size:], weights[:, rows:], preferred_element_type=jnp.float32),
        ],
        axis=1,
    )
    if state is not None:
        factor = jnp.exp(state[0] - top)
        total = total + state[1] * factor
        summed = summed + state[2] * factor
    return top, total, summed


def blocked(flat, size, rows):
    zero = jnp.zeros((size, rows), flat.dtype)
    return jnp.concatenate(
        [
            jnp.concatenate([flat[:size], zero], axis=1),
            jnp.concatenate([zero, flat[size:]], axis=1),
        ],
        axis=0,
    )


def spread(
    count,
    timestep,
    action,
    latent,
    conv_weight,
    time_table,
    action_table,
    w_qkv,
    w_out,
    stale,
    layer_out,
    fresh,
    kv,
    wq,
    wo,
    halo,
    mixed,
    normed,
    flat,
    asked,
    done,
    done_stats,
    back,
    back_stats,
    acc,
    tops,
    totals,
    modulation,
    halo_send,
    halo_recv,
    kv_send,
    kv_recv,
    relay_send,
    relay_recv,
    ask_send,
    ask_recv,
    back_send,
    back_recv,
    load_sem,
):
    rows, width = latent.shape
    size = width // HEADS
    pairs = width // LANES
    chips = count // 2
    share = width // chips
    mine = pairs // chips
    me = lax.axis_index("patch")
    core = me % 2
    chip = me // 2
    sibling = chip * 2 + (1 - core)

    def target(j):
        if chips == 4:
            return (chip, chip + 1 - 2 * (chip % 2), (chip + 2) % 4, 3 - chip)[j]
        return (chip + chips - j) % chips

    def source(j):
        if chips == 4:
            return target(j)
        return (chip + j) % chips

    loads = [
        pltpu.make_async_copy(w_qkv, wq, load_sem.at[0]),
        pltpu.make_async_copy(w_out, wo, load_sem.at[1]),
    ]
    for load in loads:
        load.start()

    barrier = pltpu.get_barrier_semaphore()
    for step in range(1, count):
        pl.semaphore_signal(
            barrier,
            inc=1,
            device_id={"patch": (me + step) % count},
            device_id_type=pl.DeviceIdType.MESH,
        )
    pl.semaphore_wait(barrier, count - 1)

    edges = []
    for slot, (start, device) in enumerate(
        ((rows - GRID_W, (me + 1) % count), (0, (me + count - 1) % count))
    ):
        copy = remote(
            latent.at[pl.ds(start, GRID_W)],
            halo.at[slot],
            halo_send.at[slot],
            halo_recv.at[slot],
            device,
        )
        copy.start()
        edges.append(copy)

    sent = []
    arriving = {}

    def piece(owner, side):
        start = pl.multiple_of(side * width + owner * share, LANES)
        return stale.at[:, pl.ds(start, share)]

    for side in range(2):
        for j in list(range(chips - 1, 0, -1)) + [0]:
            copy = remote(
                piece(target(j), side),
                kv.at[2 * j if j else 1, :, pl.ds(side * share, share)],
                kv_send.at[j, side],
                kv_recv.at[j, side],
                target(j) * 2 + core if j else sibling,
            )
            copy.start()
            sent.append(copy)
            arriving[j, side] = copy
        load = pltpu.make_async_copy(
            piece(chip, side), kv.at[0, :, pl.ds(side * share, share)], load_sem.at[2 + side]
        )
        load.start()
        loads.append(load)

    prepare(
        count, timestep, action, latent, conv_weight, time_table, action_table,
        halo, edges, mixed, normed, modulation,
    )

    loads[0].wait()
    per = CHUNK // LANES

    def project(c):
        cols = pl.ds(pl.multiple_of(c * CHUNK, CHUNK), CHUNK)
        return jnp.dot(normed[...], wq[:, cols], preferred_element_type=jnp.float32)

    def queries(c, carry):
        block = project(c) * size ** (-0.5)
        for u in range(per):
            flat[c * per + u] = jnp.transpose(block[:, u * LANES : (u + 1) * LANES]).astype(
                jnp.bfloat16
            )
        return carry

    lax.fori_loop(0, width // CHUNK, queries, 0)

    asking = []
    for j in range(1, chips):
        copy = remote(
            flat.at[pl.ds(target(j) * mine, mine)],
            asked.at[j - 1],
            ask_send.at[j - 1],
            ask_recv.at[j - 1],
            target(j) * 2 + core,
        )
        copy.start()
        sent.append(copy)
        asking.append(copy)

    def keys_values(c, carry):
        cols = pl.ds(pl.multiple_of(c * CHUNK, CHUNK), CHUNK)
        fresh[:, cols] = project(c + width // CHUNK).astype(jnp.bfloat16)
        return carry

    lax.fori_loop(0, width // CHUNK, keys_values, 0)

    relays = []
    for j in range(1, chips):
        arriving[j, 0].wait_recv()
        arriving[j, 1].wait_recv()
        copy = remote(
            kv.at[2 * j], kv.at[2 * j + 1], relay_send.at[j - 1], relay_recv.at[j - 1], sibling
        )
        copy.start()
        sent.append(copy)
        relays.append(copy)

    lax.fori_loop(width // CHUNK, 2 * width // CHUNK, keys_values, 0)

    loads[2].wait()
    loads[3].wait()
    arriving[0, 0].wait_recv()
    arriving[0, 1].wait_recv()
    for copy in relays:
        copy.wait_recv()

    def serve(j):
        slots = [slot for slot in range(count) if slot != 2 * j]
        chunks = [slots[:2], slots[2:4], slots[4:]]

        def body(i, carry):
            col = pl.multiple_of(i * LANES, LANES)
            here, there = pl.ds(col, LANES), pl.ds(pl.multiple_of(share + col, LANES), LANES)
            query = blocked(flat[chip * mine + i] if j == 0 else asked[j - 1, i], size, rows)
            state = None
            for chunk in chunks:
                keys = jnp.concatenate([kv[slot, :, here] for slot in chunk], axis=0)
                values = jnp.concatenate([kv[slot, :, there] for slot in chunk], axis=0)
                state = fold(state, keys, values, query, size, rows)
            top, total, summed = state
            result = (summed / total).astype(jnp.bfloat16)
            if j == 0:
                back[0, i] = result
                back_stats[0, pl.ds(i, 1), :] = top
                back_stats[0, pl.ds(mine + i, 1), :] = total
            else:
                done[j - 1, i] = result
                done_stats[j - 1, pl.ds(i, 1), :] = top
                done_stats[j - 1, pl.ds(mine + i, 1), :] = total
            return carry

        lax.fori_loop(0, mine, body, 0)

    serve(0)
    returning = []
    for j in range(chips - 1, 0, -1):
        asking[j - 1].wait_recv()
        serve(j)
        for n, (src, dst) in enumerate(((done, back), (done_stats, back_stats))):
            copy = remote(
                src.at[j - 1],
                dst.at[j],
                back_send.at[j - 1, n],
                back_recv.at[j - 1, n],
                source(j) * 2 + core,
            )
            copy.start()
            sent.append(copy)
            returning.append(copy)

    def local(g, carry):
        found = []
        for u in range(GROUP):
            i = g * GROUP + u
            col = pl.multiple_of(i * LANES, LANES)
            found.append(
                fold(
                    None,
                    fresh[:, pl.ds(col, LANES)],
                    fresh[:, pl.ds(pl.multiple_of(width + col, LANES), LANES)],
                    blocked(flat[i], size, rows),
                    size,
                    rows,
                )
            )
        for u in range(GROUP):
            i = g * GROUP + u
            tops[i], totals[i], acc[i] = found[u]
        return carry

    lax.fori_loop(0, pairs // GROUP, local, 0)

    def merge(j):
        def body(i, carry):
            g = target(j) * mine + i
            there = back_stats[j, pl.ds(i, 1), :]
            top = jnp.maximum(tops[g], there)
            one = jnp.exp(tops[g] - top)
            other = jnp.exp(there - top) * back_stats[j, pl.ds(mine + i, 1), :]
            total = totals[g] * one + other
            result = (acc[g] * one + back[j, i].astype(jnp.float32) * other) / total
            stacked = jnp.concatenate([result[:, :rows], result[:, rows:]], axis=0)
            cols = pl.ds(pl.multiple_of(g * LANES, LANES), LANES)
            normed[:, cols] = jnp.transpose(stacked).astype(jnp.bfloat16)
            return carry

        lax.fori_loop(0, mine, body, 0)

    merge(0)
    for j in range(chips - 1, 0, -1):
        for copy in returning[2 * (chips - 1 - j) : 2 * (chips - j)]:
            copy.wait_recv()
        merge(j)
    loads[1].wait()

    def output(c, carry):
        cols = pl.ds(pl.multiple_of(c * CHUNK, CHUNK), CHUNK)
        proj = jnp.dot(normed[...], wo[:, cols], preferred_element_type=jnp.float32)
        gate = modulation[:, pl.ds(pl.multiple_of(2 * width + c * CHUNK, CHUNK), CHUNK)]
        layer_out[:, cols] = (mixed[:, cols] + gate * proj).astype(jnp.bfloat16)
        return carry

    lax.fori_loop(0, width // CHUNK, output, 0)

    for copy in edges + sent:
        copy.wait_send()


def per_device(
    count, latent, conv_weight, time_table, action_table, timestep, action, w_qkv, w_out, stale_kv
):
    rows, width = latent.shape
    pairs = width // LANES
    size = width // HEADS
    chips = count // 2
    vmem = pl.BlockSpec(memory_space=pltpu.VMEM)
    smem = pl.BlockSpec(memory_space=pltpu.SMEM)
    anywhere = pl.BlockSpec(memory_space=pl.ANY)
    dma = pltpu.SemaphoreType.DMA
    front = [
        pltpu.VMEM(w_qkv.shape, jnp.bfloat16),
        pltpu.VMEM(w_out.shape, jnp.bfloat16),
        pltpu.VMEM((2, GRID_W, width), jnp.bfloat16),
        pltpu.VMEM((rows, width), jnp.float32),
        pltpu.VMEM((rows, width), jnp.bfloat16),
    ]
    state = [
        pltpu.VMEM((pairs, size, 2 * rows), jnp.float32),
        pltpu.VMEM((pairs, 1, 2 * rows), jnp.float32),
        pltpu.VMEM((pairs, 1, 2 * rows), jnp.float32),
        pltpu.VMEM((1, 3 * width), jnp.float32),
        dma((2,)),
        dma((2,)),
        dma((chips, 2)),
    ]
    if pairs % chips == 0 and width % (chips * LANES) == 0:
        body = spread
        mine = pairs // chips
        lines = 8 * pl.cdiv(2 * mine, 8)
        scratch = [
            pltpu.VMEM((count, rows, 2 * width // chips), jnp.bfloat16),
            *front,
            pltpu.VMEM((pairs, LANES, rows), jnp.bfloat16),
            pltpu.VMEM((chips - 1, mine, LANES, rows), jnp.bfloat16),
            pltpu.VMEM((chips - 1, mine, size, 2 * rows), jnp.bfloat16),
            pltpu.VMEM((chips - 1, lines, 2 * rows), jnp.float32),
            pltpu.VMEM((chips, mine, size, 2 * rows), jnp.bfloat16),
            pltpu.VMEM((chips, lines, 2 * rows), jnp.float32),
            *state,
            dma((chips, 2)),
            dma((chips - 1,)),
            dma((chips - 1,)),
            dma((chips - 1,)),
            dma((chips - 1,)),
            dma((chips - 1, 2)),
            dma((chips - 1, 2)),
            dma((4,)),
        ]
    else:
        body = kernel
        scratch = [
            pltpu.VMEM((count - 1, rows, 2 * width), jnp.bfloat16),
            *front,
            pltpu.VMEM((pairs, LANES, 2 * rows), jnp.bfloat16),
            *state,
            dma((chips - 1, 2)),
            dma((2,)),
            dma((count - 1, 2)),
            dma((2,)),
        ]
    return pl.pallas_call(
        functools.partial(body, count),
        out_shape=(
            jax.ShapeDtypeStruct((rows, width), jnp.bfloat16),
            jax.ShapeDtypeStruct((rows, 2 * width), jnp.bfloat16),
        ),
        in_specs=[smem, smem, vmem, vmem, vmem, vmem, anywhere, anywhere, anywhere],
        out_specs=(vmem, vmem),
        scratch_shapes=scratch,
        compiler_params=pltpu.CompilerParams(
            collective_id=0, has_side_effects=True, vmem_limit_bytes=60 * 2**20
        ),
        cost_estimate=pl.CostEstimate(
            flops=8 * 10**9, bytes_accessed=30 * 2**20, transcendentals=13 * 10**6
        ),
    )(timestep, action, latent, conv_weight, time_table, action_table, w_qkv, w_out, stale_kv)


def solution(mesh):
    in_specs = (
        P(("frame", "patch"), None),
        P(),
        P(),
        P(),
        P("frame"),
        P("frame"),
        P(),
        P(),
        P(("frame", "patch"), None),
    )
    out_specs = (P(("frame", "patch"), None), P(("frame", "patch"), None))
    return jax.shard_map(
        functools.partial(per_device, mesh.shape["patch"]),
        mesh=mesh,
        in_specs=in_specs,
        out_specs=out_specs,
        check_vma=False,
    )
```

```python
import functools

import jax
import jax.numpy as jnp
from jax import lax
from jax.experimental import pallas as pl
from jax.experimental.pallas import tpu as pltpu
from jax.sharding import PartitionSpec as P

HEADS = 24
GRID_W = 64
LANES = 128
GROUP = 2
MANY = 4
CHUNK = 512


def prepare(
    count,
    timestep,
    action,
    latent,
    conv_weight,
    time_table,
    action_table,
    halo,
    edges,
    mixed,
    normed,
    modulation,
):
    rows, width = latent.shape
    me = lax.axis_index("patch")

    def pick(table, index):
        hot = lax.broadcasted_iota(jnp.int32, table.shape, 0) == index
        return jnp.sum(
            jnp.where(hot, table[...].astype(jnp.float32), 0.0), axis=0, keepdims=True
        )

    modulation[...] = pick(time_table, timestep[0]) + pick(action_table, action[0])

    nrows = rows // GRID_W

    def stem(r):
        def body(c, carry):
            cols = pl.ds(pl.multiple_of(c * 2 * LANES, 2 * LANES), 2 * LANES)
            taps = conv_weight[:, cols]
            lines = []
            for a in (r - 1, r, r + 1):
                if a < 0:
                    line = jnp.where(me > 0, halo[0, :, cols].astype(jnp.float32), 0.0)
                elif a >= nrows:
                    line = jnp.where(me < count - 1, halo[1, :, cols].astype(jnp.float32), 0.0)
                else:
                    line = latent[pl.ds(a * GRID_W, GRID_W), cols].astype(jnp.float32)
                lines.append(line)
            sums = []
            for b in range(3):
                total = lines[0] * taps[b : b + 1]
                total = total + lines[1] * taps[3 + b : 4 + b]
                sums.append(total + lines[2] * taps[6 + b : 7 + b])
            place = lax.broadcasted_iota(jnp.int32, sums[0].shape, 0)
            before = jnp.where(place == 0, 0.0, pltpu.roll(sums[0], 1, 0))
            after = jnp.where(place == GRID_W - 1, 0.0, pltpu.roll(sums[2], GRID_W - 1, 0))
            mixed[pl.ds(r * GRID_W, GRID_W), cols] = lines[1] + sums[1] + (before + after)
            return carry

        lax.fori_loop(0, width // (2 * LANES), body, 0)

    for r in range(1, nrows - 1):
        stem(r)
    for edge in edges:
        edge.wait_recv()
    stem(0)
    stem(nrows - 1)

    def norm(r, carry):
        span = pl.ds(pl.multiple_of(r * 32, 32), 32)
        x = mixed[span, :]
        mean = jnp.mean(x, axis=1, keepdims=True)
        centred = x - mean
        var = jnp.mean(centred * centred, axis=1, keepdims=True)
        gain = 1.0 + modulation[:, width : 2 * width]
        normed[span, :] = (
            centred * lax.rsqrt(var + 1e-06) * gain + modulation[:, :width]
        ).astype(jnp.bfloat16)
        return carry

    lax.fori_loop(0, rows // 32, norm, 0)


def kernel(
    count,
    timestep,
    action,
    latent,
    conv_weight,
    time_table,
    action_table,
    w_qkv,
    w_out,
    stale,
    layer_out,
    fresh,
    kv,
    wq,
    wo,
    halo,
    mixed,
    normed,
    qbd,
    acc,
    tops,
    totals,
    modulation,
    halo_send,
    halo_recv,
    own_send,
    relay_send,
    cross_send,
    recv,
    load_sem,
):
    rows, width = latent.shape
    half = rows // 2
    size = width // HEADS
    pairs = width // LANES
    chips = count // 2
    me = lax.axis_index("patch")
    core = me % 2
    chip = me // 2
    sibling = chip * 2 + (1 - core)

    def part(h):
        return pl.ds(h * half, half)

    def target(j):
        if chips == 4:
            other = chip + 1 - 2 * (chip % 2) if j == 1 else (chip + 2) % 4
        else:
            other = (chip + chips - j) % chips
        return other * 2 + core

    def send(src, role, h, sem, device):
        copy = pltpu.make_async_remote_copy(
            src_ref=src,
            dst_ref=kv.at[role - 1, part(h)],
            send_sem=sem,
            recv_sem=recv.at[role - 1, h],
            device_id={"patch": device},
            device_id_type=pl.DeviceIdType.MESH,
        )
        copy.start()
        return copy

    def arrived(role, h):
        pltpu.make_async_remote_copy(
            src_ref=kv.at[role - 1, part(h)],
            dst_ref=kv.at[role - 1, part(h)],
            send_sem=cross_send.at[0],
            recv_sem=recv.at[role - 1, h],
            device_id={"patch": sibling},
            device_id_type=pl.DeviceIdType.MESH,
        ).wait_recv()

    loads = [
        pltpu.make_async_copy(w_qkv, wq, load_sem.at[0]),
        pltpu.make_async_copy(w_out, wo, load_sem.at[1]),
    ]
    for load in loads:
        load.start()

    barrier = pltpu.get_barrier_semaphore()
    for step in range(1, count):
        pl.semaphore_signal(
            barrier,
            inc=1,
            device_id={"patch": (me + step) % count},
            device_id_type=pl.DeviceIdType.MESH,
        )
    pl.semaphore_wait(barrier, count - 1)

    edges = []
    for slot, (start, device) in enumerate(
        ((rows - GRID_W, (me + 1) % count), (0, (me + count - 1) % count))
    ):
        copy = pltpu.make_async_remote_copy(
            src_ref=latent.at[pl.ds(start, GRID_W)],
            dst_ref=halo.at[slot],
            send_sem=halo_send.at[slot],
            recv_sem=halo_recv.at[slot],
            device_id={"patch": device},
            device_id_type=pl.DeviceIdType.MESH,
        )
        copy.start()
        edges.append(copy)

    sent = []
    direct = (1, 2) if chips == 4 else tuple(range(1, chips))
    for order in range(2):
        for j in direct:
            h = order if j % 2 == 1 else 1 - order
            sent.append(send(stale.at[part(h)], 2 * j, h, own_send.at[j, h], target(j)))
        sent.append(send(stale.at[part(order)], 1, order, own_send.at[0, order], sibling))

    def relay(j, h):
        arrived(2 * j, h)
        if chips == 4 and (j, h) == (1, 0):
            sent.append(send(kv.at[1, part(0)], 6, 0, cross_send.at[0], target(2)))
        if chips == 4 and (j, h) == (2, 1):
            sent.append(send(kv.at[3, part(1)], 6, 1, cross_send.at[1], target(1)))
        sent.append(
            send(kv.at[2 * j - 1, part(h)], 2 * j + 1, h, relay_send.at[j - 1, h], sibling)
        )

    prepare(
        count, timestep, action, latent, conv_weight, time_table, action_table,
        halo, edges, mixed, normed, modulation,
    )

    loads[0].wait()
    qbd[...] = jnp.zeros_like(qbd)
    per = CHUNK // LANES

    def project(c):
        cols = pl.ds(pl.multiple_of(c * CHUNK, CHUNK), CHUNK)
        return jnp.dot(normed[...], wq[:, cols], preferred_element_type=jnp.float32)

    def queries(c, carry):
        block = project(c) * size ** (-0.5)
        for u in range(per):
            flipped = jnp.transpose(block[:, u * LANES : (u + 1) * LANES]).astype(jnp.bfloat16)
            qbd[c * per + u, :size, :rows] = flipped[:size]
            qbd[c * per + u, size:, rows:] = flipped[size:]
        return carry

    lax.fori_loop(0, width // CHUNK, queries, 0)

    def keys_values(c, carry):
        cols = pl.ds(pl.multiple_of(c * CHUNK, CHUNK), CHUNK)
        fresh[:, cols] = project(c + width // CHUNK).astype(jnp.bfloat16)
        return carry

    lax.fori_loop(0, 2 * width // CHUNK, keys_values, 0)

    def attend(read, first=False):
        def body(g, carry):
            done = []
            for u in range(GROUP):
                i = g * GROUP + u
                col = pl.multiple_of(i * LANES, LANES)
                scores = jnp.dot(
                    read(pl.ds(col, LANES)), qbd[i], preferred_element_type=jnp.float32
                )
                top = jnp.max(scores, axis=0, keepdims=True)
                if not first:
                    top = jnp.maximum(top, tops[i])
                expo = jnp.exp(scores - top)
                total = jnp.sum(expo, axis=0, keepdims=True)
                weights = expo.astype(jnp.bfloat16)
                flipped = jnp.transpose(read(pl.ds(pl.multiple_of(width + col, LANES), LANES)))
                summed = jnp.concatenate(
                    [
                        jnp.dot(
                            flipped[:size], weights[:, :rows], preferred_element_type=jnp.float32
                        ),
                        jnp.dot(
                            flipped[size:], weights[:, rows:], preferred_element_type=jnp.float32
                        ),
                    ],
                    axis=1,
                )
                if not first:
                    factor = jnp.exp(tops[i] - top)
                    total = total + totals[i] * factor
                    summed = summed + acc[i] * factor
                done.append((i, top, total, summed))
            for i, top, total, summed in done:
                tops[i] = top
                totals[i] = total
                acc[i] = summed
            return carry

        lax.fori_loop(0, pairs // GROUP, body, 0)

    def landed(pieces):
        def read(cols):
            return jnp.concatenate(
                [kv[role - 1, part(h), cols] for role, h in pieces], axis=0
            )

        return read

    arrived(1, 0)
    arrived(1, 1)
    beside = landed([(1, 0), (1, 1)])
    attend(lambda cols: jnp.concatenate([fresh[:, cols], beside(cols)], axis=0), first=True)
    if chips == 4:
        plan = [((1, 0), (2, 1)), ((1, 1), (2, 0)), ((3, 0), (3, 1))]
    else:
        plan = [((j, 0), (j, 1)) for j in range(1, chips)]
    for pair in plan:
        for j, h in pair:
            relay(j, h)
        for j, h in pair:
            arrived(2 * j + 1, h)
        attend(landed([(2 * j + c, h) for j, h in pair for c in range(2)]))

    def finish(i, carry):
        result = acc[i] / totals[i]
        stacked = jnp.concatenate([result[:, :rows], result[:, rows:]], axis=0)
        cols = pl.ds(pl.multiple_of(i * LANES, LANES), LANES)
        normed[:, cols] = jnp.transpose(stacked).astype(jnp.bfloat16)
        return carry

    lax.fori_loop(0, pairs, finish, 0)
    loads[1].wait()

    def output(c, carry):
        cols = pl.ds(pl.multiple_of(c * CHUNK, CHUNK), CHUNK)
        proj = jnp.dot(normed[...], wo[:, cols], preferred_element_type=jnp.float32)
        gate = modulation[:, pl.ds(pl.multiple_of(2 * width + c * CHUNK, CHUNK), CHUNK)]
        layer_out[:, cols] = (mixed[:, cols] + gate * proj).astype(jnp.bfloat16)
        return carry

    lax.fori_loop(0, width // CHUNK, output, 0)

    for copy in edges + sent:
        copy.wait_send()


def remote(src, dst, send_sem, recv_sem, device):
    return pltpu.make_async_remote_copy(
        src_ref=src,
        dst_ref=dst,
        send_sem=send_sem,
        recv_sem=recv_sem,
        device_id={"patch": device},
        device_id_type=pl.DeviceIdType.MESH,
    )


def fold(state, scores, flipped, size, rows):
    top = jnp.max(scores, axis=0, keepdims=True)
    if state is not None:
        top = jnp.maximum(top, state[0])
    expo = jnp.exp(scores - top)
    total = jnp.sum(expo, axis=0, keepdims=True)
    weights = expo.astype(jnp.bfloat16)
    summed = jnp.concatenate(
        [
            jnp.dot(flipped[:size], weights[:, :rows], preferred_element_type=jnp.float32),
            jnp.dot(flipped[size:], weights[:, rows:], preferred_element_type=jnp.float32),
        ],
        axis=1,
    )
    if state is not None:
        factor = jnp.exp(state[0] - top)
        total = total + state[1] * factor
        summed = summed + state[2] * factor
    return top, total, summed


def pipeline(tasks, size, rows):
    states = {}
    waiting = None
    for task in tasks + [None]:
        ahead = None
        if task is not None:
            ahead = jnp.dot(task[1](), task[3], preferred_element_type=jnp.float32)
        if waiting is not None:
            (stream, _, values, _), scores = waiting
            states[stream] = fold(states.get(stream), scores, values(), size, rows)
        waiting = (task, ahead)
    return states


def blocked(flat, size, rows):
    zero = jnp.zeros((size, rows), flat.dtype)
    return jnp.concatenate(
        [
            jnp.concatenate([flat[:size], zero], axis=1),
            jnp.concatenate([zero, flat[size:]], axis=1),
        ],
        axis=0,
    )


def spread(
    count,
    timestep,
    action,
    latent,
    conv_weight,
    time_table,
    action_table,
    w_qkv,
    w_out,
    stale,
    layer_out,
    fresh,
    kv,
    wq,
    wo,
    halo,
    mixed,
    normed,
    flat,
    turned,
    asked,
    done,
    done_stats,
    back,
    back_stats,
    acc,
    tops,
    totals,
    modulation,
    halo_send,
    halo_recv,
    kv_send,
    kv_recv,
    relay_send,
    relay_recv,
    ask_send,
    ask_recv,
    back_send,
    back_recv,
    load_sem,
):
    rows, width = latent.shape
    size = width // HEADS
    pairs = width // LANES
    chips = count // 2
    share = width // chips
    mine = pairs // chips
    me = lax.axis_index("patch")
    core = me % 2
    chip = me // 2
    sibling = chip * 2 + (1 - core)

    def target(j):
        if chips == 4:
            return (chip, chip + 1 - 2 * (chip % 2), (chip + 2) % 4, 3 - chip)[j]
        return (chip + chips - j) % chips

    def source(j):
        if chips == 4:
            return target(j)
        return (chip + j) % chips

    loads = [
        pltpu.make_async_copy(w_qkv, wq, load_sem.at[0]),
        pltpu.make_async_copy(w_out, wo, load_sem.at[1]),
    ]
    for load in loads:
        load.start()

    barrier = pltpu.get_barrier_semaphore()
    for step in range(1, count):
        pl.semaphore_signal(
            barrier,
            inc=1,
            device_id={"patch": (me + step) % count},
            device_id_type=pl.DeviceIdType.MESH,
        )
    pl.semaphore_wait(barrier, count - 1)

    edges = []
    for slot, (start, device) in enumerate(
        ((rows - GRID_W, (me + 1) % count), (0, (me + count - 1) % count))
    ):
        copy = remote(
            latent.at[pl.ds(start, GRID_W)],
            halo.at[slot],
            halo_send.at[slot],
            halo_recv.at[slot],
            device,
        )
        copy.start()
        edges.append(copy)

    sent = []
    arriving = {}

    def piece(owner, side):
        start = pl.multiple_of(side * width + owner * share, LANES)
        return stale.at[:, pl.ds(start, share)]

    for side in range(2):
        for j in list(range(chips - 1, 0, -1)) + [0]:
            copy = remote(
                piece(target(j), side),
                kv.at[2 * j if j else 1, :, pl.ds(side * share, share)],
                kv_send.at[j, side],
                kv_recv.at[j, side],
                target(j) * 2 + core if j else sibling,
            )
            copy.start()
            sent.append(copy)
            arriving[j, side] = copy
        load = pltpu.make_async_copy(
            piece(chip, side), kv.at[0, :, pl.ds(side * share, share)], load_sem.at[2 + side]
        )
        load.start()
        loads.append(load)

    prepare(
        count, timestep, action, latent, conv_weight, time_table, action_table,
        halo, edges, mixed, normed, modulation,
    )

    loads[0].wait()
    per = CHUNK // LANES

    def project(c):
        cols = pl.ds(pl.multiple_of(c * CHUNK, CHUNK), CHUNK)
        return jnp.dot(normed[...], wq[:, cols], preferred_element_type=jnp.float32)

    def queries(c, carry):
        block = project(c) * size ** (-0.5)
        for u in range(per):
            flat[c * per + u] = jnp.transpose(block[:, u * LANES : (u + 1) * LANES]).astype(
                jnp.bfloat16
            )
        return carry

    lax.fori_loop(0, width // CHUNK, queries, 0)

    asking = []
    for j in range(1, chips):
        copy = remote(
            flat.at[pl.ds(target(j) * mine, mine)],
            asked.at[j - 1],
            ask_send.at[j - 1],
            ask_recv.at[j - 1],
            target(j) * 2 + core,
        )
        copy.start()
        sent.append(copy)
        asking.append(copy)

    def keys_values(c, carry):
        cols = pl.ds(pl.multiple_of(c * CHUNK, CHUNK), CHUNK)
        fresh[:, cols] = project(c + width // CHUNK).astype(jnp.bfloat16)
        return carry

    lax.fori_loop(0, 2 * width // CHUNK, keys_values, 0)

    def local(g, carry):
        def read(start):
            return fresh[:, pl.ds(pl.multiple_of(start, LANES), LANES)]

        def task(u):
            i = g * MANY + u
            return (
                u,
                lambda: read(i * LANES),
                lambda: jnp.transpose(read(width + i * LANES)),
                blocked(flat[i], size, rows),
            )

        found = pipeline([task(u) for u in range(MANY)], size, rows)
        for u in range(MANY):
            i = g * MANY + u
            tops[i], totals[i], acc[i] = found[u]
        return carry

    early = pairs // MANY - 1

    lax.fori_loop(0, early, local, 0)

    relays = []
    for j in range(1, chips):
        arriving[j, 0].wait_recv()
        arriving[j, 1].wait_recv()
        copy = remote(
            kv.at[2 * j], kv.at[2 * j + 1], relay_send.at[j - 1], relay_recv.at[j - 1], sibling
        )
        copy.start()
        sent.append(copy)
        relays.append(copy)

    def turn(slot, carry):
        for i in range(mine):
            turned[i, :, pl.ds(pl.multiple_of(slot * rows, rows), rows)] = jnp.transpose(
                kv[slot, :, pl.ds(share + i * LANES, LANES)]
            )
        return carry

    loads[2].wait()
    loads[3].wait()
    arriving[0, 0].wait_recv()
    arriving[0, 1].wait_recv()
    turn(1, 0)
    lax.fori_loop(0, chips, lambda n, carry: turn(2 * n, carry), 0)
    for copy in relays:
        copy.wait_recv()
    lax.fori_loop(1, chips, lambda n, carry: turn(2 * n + 1, carry), 0)

    def serve(j):
        slots = [slot for slot in range(count) if slot != 2 * j]
        chunks = [slots[n : n + 2] for n in range(0, count - 4, 2)] + [slots[count - 4 :]]
        queries = [
            blocked(flat[chip * mine + i] if j == 0 else asked[j - 1, i], size, rows)
            for i in range(mine)
        ]

        def keys(chunk, i):
            cols = pl.ds(i * LANES, LANES)
            return lambda: jnp.concatenate([kv[slot, :, cols] for slot in chunk], axis=0)

        def values(chunk, i):
            return lambda: jnp.concatenate(
                [turned[i, :, pl.ds(slot * rows, rows)] for slot in chunk], axis=1
            )

        tasks = [
            (i, keys(chunk, i), values(chunk, i), queries[i])
            for chunk in chunks
            for i in range(mine)
        ]
        for i, (top, total, summed) in pipeline(tasks, size, rows).items():
            result = (summed / total).astype(jnp.bfloat16)
            place, stats = (back.at[0], back_stats.at[0])
            if j > 0:
                place, stats = (done.at[j - 1], done_stats.at[j - 1])
            place[i] = result
            stats[i : i + 1, :] = top
            stats[mine + i : mine + i + 1, :] = total

    serve(0)
    returning = []
    for j in range(chips - 1, 0, -1):
        asking[j - 1].wait_recv()
        serve(j)
        for n, (src, dst) in enumerate(((done, back), (done_stats, back_stats))):
            copy = remote(
                src.at[j - 1],
                dst.at[j],
                back_send.at[j - 1, n],
                back_recv.at[j - 1, n],
                source(j) * 2 + core,
            )
            copy.start()
            sent.append(copy)
            returning.append(copy)

    lax.fori_loop(early, pairs // MANY, local, 0)

    def merge(j):
        def body(i, carry):
            g = target(j) * mine + i
            there = back_stats[j, pl.ds(i, 1), :]
            top = jnp.maximum(tops[g], there)
            one = jnp.exp(tops[g] - top)
            other = jnp.exp(there - top) * back_stats[j, pl.ds(mine + i, 1), :]
            total = totals[g] * one + other
            result = (acc[g] * one + back[j, i].astype(jnp.float32) * other) / total
            stacked = jnp.concatenate([result[:, :rows], result[:, rows:]], axis=0)
            cols = pl.ds(pl.multiple_of(g * LANES, LANES), LANES)
            normed[:, cols] = jnp.transpose(stacked).astype(jnp.bfloat16)
            return carry

        lax.fori_loop(0, mine, body, 0)

    merge(0)
    for j in range(chips - 1, 0, -1):
        for copy in returning[2 * (chips - 1 - j) : 2 * (chips - j)]:
            copy.wait_recv()
        merge(j)
    loads[1].wait()

    def output(c, carry):
        cols = pl.ds(pl.multiple_of(c * CHUNK, CHUNK), CHUNK)
        proj = jnp.dot(normed[...], wo[:, cols], preferred_element_type=jnp.float32)
        gate = modulation[:, pl.ds(pl.multiple_of(2 * width + c * CHUNK, CHUNK), CHUNK)]
        layer_out[:, cols] = (mixed[:, cols] + gate * proj).astype(jnp.bfloat16)
        return carry

    lax.fori_loop(0, width // CHUNK, output, 0)

    for copy in edges + sent:
        copy.wait_send()


def per_device(
    count, latent, conv_weight, time_table, action_table, timestep, action, w_qkv, w_out, stale_kv
):
    rows, width = latent.shape
    pairs = width // LANES
    size = width // HEADS
    chips = count // 2
    vmem = pl.BlockSpec(memory_space=pltpu.VMEM)
    smem = pl.BlockSpec(memory_space=pltpu.SMEM)
    anywhere = pl.BlockSpec(memory_space=pl.ANY)
    dma = pltpu.SemaphoreType.DMA
    front = [
        pltpu.VMEM(w_qkv.shape, jnp.bfloat16),
        pltpu.VMEM(w_out.shape, jnp.bfloat16),
        pltpu.VMEM((2, GRID_W, width), jnp.bfloat16),
        pltpu.VMEM((rows, width), jnp.float32),
        pltpu.VMEM((rows, width), jnp.bfloat16),
    ]
    state = [
        pltpu.VMEM((pairs, size, 2 * rows), jnp.float32),
        pltpu.VMEM((pairs, 1, 2 * rows), jnp.float32),
        pltpu.VMEM((pairs, 1, 2 * rows), jnp.float32),
        pltpu.VMEM((1, 3 * width), jnp.float32),
        dma((2,)),
        dma((2,)),
        dma((chips, 2)),
    ]
    if pairs % chips == 0 and width % (chips * LANES) == 0:
        body = spread
        mine = pairs // chips
        lines = 8 * pl.cdiv(2 * mine, 8)
        scratch = [
            pltpu.VMEM((count, rows, 2 * width // chips), jnp.bfloat16),
            *front,
            pltpu.VMEM((pairs, LANES, rows), jnp.bfloat16),
            pltpu.VMEM((mine, LANES, count * rows), jnp.bfloat16),
            pltpu.VMEM((chips - 1, mine, LANES, rows), jnp.bfloat16),
            pltpu.VMEM((chips - 1, mine, size, 2 * rows), jnp.bfloat16),
            pltpu.VMEM((chips - 1, lines, 2 * rows), jnp.float32),
            pltpu.VMEM((chips, mine, size, 2 * rows), jnp.bfloat16),
            pltpu.VMEM((chips, lines, 2 * rows), jnp.float32),
            *state,
            dma((chips, 2)),
            dma((chips - 1,)),
            dma((chips - 1,)),
            dma((chips - 1,)),
            dma((chips - 1,)),
            dma((chips - 1, 2)),
            dma((chips - 1, 2)),
            dma((4,)),
        ]
    else:
        body = kernel
        scratch = [
            pltpu.VMEM((count - 1, rows, 2 * width), jnp.bfloat16),
            *front,
            pltpu.VMEM((pairs, LANES, 2 * rows), jnp.bfloat16),
            *state,
            dma((chips - 1, 2)),
            dma((2,)),
            dma((count - 1, 2)),
            dma((2,)),
        ]
    return pl.pallas_call(
        functools.partial(body, count),
        out_shape=(
            jax.ShapeDtypeStruct((rows, width), jnp.bfloat16),
            jax.ShapeDtypeStruct((rows, 2 * width), jnp.bfloat16),
        ),
        in_specs=[smem, smem, vmem, vmem, vmem, vmem, anywhere, anywhere, anywhere],
        out_specs=(vmem, vmem),
        scratch_shapes=scratch,
        compiler_params=pltpu.CompilerParams(
            collective_id=0, has_side_effects=True, vmem_limit_bytes=60 * 2**20
        ),
        cost_estimate=pl.CostEstimate(
            flops=8 * 10**9, bytes_accessed=30 * 2**20, transcendentals=13 * 10**6
        ),
    )(timestep, action, latent, conv_weight, time_table, action_table, w_qkv, w_out, stale_kv)


def solution(mesh):
    in_specs = (
        P(("frame", "patch"), None),
        P(),
        P(),
        P(),
        P("frame"),
        P("frame"),
        P(),
        P(),
        P(("frame", "patch"), None),
    )
    out_specs = (P(("frame", "patch"), None), P(("frame", "patch"), None))
    return jax.shard_map(
        functools.partial(per_device, mesh.shape["patch"]),
        mesh=mesh,
        in_specs=in_specs,
        out_specs=out_specs,
        check_vma=False,
    )
```

```python
import functools

import jax
import jax.numpy as jnp
from jax import lax
from jax.experimental import pallas as pl
from jax.experimental.pallas import tpu as pltpu
from jax.sharding import PartitionSpec as P

HEADS = 24
GRID_W = 64
LANES = 128
GROUP = 2
MANY = 4
CHUNK = 512


def prepare(
    count,
    timestep,
    action,
    latent,
    conv_weight,
    time_table,
    action_table,
    halo,
    edges,
    mixed,
    normed,
    modulation,
):
    rows, width = latent.shape
    me = lax.axis_index("patch")

    def pick(table, index):
        hot = lax.broadcasted_iota(jnp.int32, table.shape, 0) == index
        return jnp.sum(
            jnp.where(hot, table[...].astype(jnp.float32), 0.0), axis=0, keepdims=True
        )

    modulation[...] = pick(time_table, timestep[0]) + pick(action_table, action[0])

    nrows = rows // GRID_W

    def stem(r):
        def body(c, carry):
            cols = pl.ds(pl.multiple_of(c * 2 * LANES, 2 * LANES), 2 * LANES)
            taps = conv_weight[:, cols]
            lines = []
            for a in (r - 1, r, r + 1):
                if a < 0:
                    line = jnp.where(me > 0, halo[0, :, cols].astype(jnp.float32), 0.0)
                elif a >= nrows:
                    line = jnp.where(me < count - 1, halo[1, :, cols].astype(jnp.float32), 0.0)
                else:
                    line = latent[pl.ds(a * GRID_W, GRID_W), cols].astype(jnp.float32)
                lines.append(line)
            sums = []
            for b in range(3):
                total = lines[0] * taps[b : b + 1]
                total = total + lines[1] * taps[3 + b : 4 + b]
                sums.append(total + lines[2] * taps[6 + b : 7 + b])
            place = lax.broadcasted_iota(jnp.int32, sums[0].shape, 0)
            before = jnp.where(place == 0, 0.0, pltpu.roll(sums[0], 1, 0))
            after = jnp.where(place == GRID_W - 1, 0.0, pltpu.roll(sums[2], GRID_W - 1, 0))
            mixed[pl.ds(r * GRID_W, GRID_W), cols] = lines[1] + sums[1] + (before + after)
            return carry

        lax.fori_loop(0, width // (2 * LANES), body, 0)

    for r in range(1, nrows - 1):
        stem(r)
    for edge in edges:
        edge.wait_recv()
    stem(0)
    stem(nrows - 1)

    def norm(r, carry):
        span = pl.ds(pl.multiple_of(r * 32, 32), 32)
        x = mixed[span, :]
        mean = jnp.mean(x, axis=1, keepdims=True)
        centred = x - mean
        var = jnp.mean(centred * centred, axis=1, keepdims=True)
        gain = 1.0 + modulation[:, width : 2 * width]
        normed[span, :] = (
            centred * lax.rsqrt(var + 1e-06) * gain + modulation[:, :width]
        ).astype(jnp.bfloat16)
        return carry

    lax.fori_loop(0, rows // 32, norm, 0)


def kernel(
    count,
    timestep,
    action,
    latent,
    conv_weight,
    time_table,
    action_table,
    w_qkv,
    w_out,
    stale,
    layer_out,
    fresh,
    kv,
    wq,
    wo,
    halo,
    mixed,
    normed,
    qbd,
    acc,
    tops,
    totals,
    modulation,
    halo_send,
    halo_recv,
    own_send,
    relay_send,
    cross_send,
    recv,
    load_sem,
):
    rows, width = latent.shape
    half = rows // 2
    size = width // HEADS
    pairs = width // LANES
    chips = count // 2
    me = lax.axis_index("patch")
    core = me % 2
    chip = me // 2
    sibling = chip * 2 + (1 - core)

    def part(h):
        return pl.ds(h * half, half)

    def target(j):
        if chips == 4:
            other = chip + 1 - 2 * (chip % 2) if j == 1 else (chip + 2) % 4
        else:
            other = (chip + chips - j) % chips
        return other * 2 + core

    def send(src, role, h, sem, device):
        copy = pltpu.make_async_remote_copy(
            src_ref=src,
            dst_ref=kv.at[role - 1, part(h)],
            send_sem=sem,
            recv_sem=recv.at[role - 1, h],
            device_id={"patch": device},
            device_id_type=pl.DeviceIdType.MESH,
        )
        copy.start()
        return copy

    def arrived(role, h):
        pltpu.make_async_remote_copy(
            src_ref=kv.at[role - 1, part(h)],
            dst_ref=kv.at[role - 1, part(h)],
            send_sem=cross_send.at[0],
            recv_sem=recv.at[role - 1, h],
            device_id={"patch": sibling},
            device_id_type=pl.DeviceIdType.MESH,
        ).wait_recv()

    loads = [
        pltpu.make_async_copy(w_qkv, wq, load_sem.at[0]),
        pltpu.make_async_copy(w_out, wo, load_sem.at[1]),
    ]
    for load in loads:
        load.start()

    barrier = pltpu.get_barrier_semaphore()
    for step in range(1, count):
        pl.semaphore_signal(
            barrier,
            inc=1,
            device_id={"patch": (me + step) % count},
            device_id_type=pl.DeviceIdType.MESH,
        )
    pl.semaphore_wait(barrier, count - 1)

    edges = []
    for slot, (start, device) in enumerate(
        ((rows - GRID_W, (me + 1) % count), (0, (me + count - 1) % count))
    ):
        copy = pltpu.make_async_remote_copy(
            src_ref=latent.at[pl.ds(start, GRID_W)],
            dst_ref=halo.at[slot],
            send_sem=halo_send.at[slot],
            recv_sem=halo_recv.at[slot],
            device_id={"patch": device},
            device_id_type=pl.DeviceIdType.MESH,
        )
        copy.start()
        edges.append(copy)

    sent = []
    direct = (1, 2) if chips == 4 else tuple(range(1, chips))
    for order in range(2):
        for j in direct:
            h = order if j % 2 == 1 else 1 - order
            sent.append(send(stale.at[part(h)], 2 * j, h, own_send.at[j, h], target(j)))
        sent.append(send(stale.at[part(order)], 1, order, own_send.at[0, order], sibling))

    def relay(j, h):
        arrived(2 * j, h)
        if chips == 4 and (j, h) == (1, 0):
            sent.append(send(kv.at[1, part(0)], 6, 0, cross_send.at[0], target(2)))
        if chips == 4 and (j, h) == (2, 1):
            sent.append(send(kv.at[3, part(1)], 6, 1, cross_send.at[1], target(1)))
        sent.append(
            send(kv.at[2 * j - 1, part(h)], 2 * j + 1, h, relay_send.at[j - 1, h], sibling)
        )

    prepare(
        count, timestep, action, latent, conv_weight, time_table, action_table,
        halo, edges, mixed, normed, modulation,
    )

    loads[0].wait()
    qbd[...] = jnp.zeros_like(qbd)
    per = CHUNK // LANES

    def project(c):
        cols = pl.ds(pl.multiple_of(c * CHUNK, CHUNK), CHUNK)
        return jnp.dot(normed[...], wq[:, cols], preferred_element_type=jnp.float32)

    def queries(c, carry):
        block = project(c) * size ** (-0.5)
        for u in range(per):
            flipped = jnp.transpose(block[:, u * LANES : (u + 1) * LANES]).astype(jnp.bfloat16)
            qbd[c * per + u, :size, :rows] = flipped[:size]
            qbd[c * per + u, size:, rows:] = flipped[size:]
        return carry

    lax.fori_loop(0, width // CHUNK, queries, 0)

    def keys_values(c, carry):
        cols = pl.ds(pl.multiple_of(c * CHUNK, CHUNK), CHUNK)
        fresh[:, cols] = project(c + width // CHUNK).astype(jnp.bfloat16)
        return carry

    lax.fori_loop(0, 2 * width // CHUNK, keys_values, 0)

    def attend(read, first=False):
        def body(g, carry):
            done = []
            for u in range(GROUP):
                i = g * GROUP + u
                col = pl.multiple_of(i * LANES, LANES)
                scores = jnp.dot(
                    read(pl.ds(col, LANES)), qbd[i], preferred_element_type=jnp.float32
                )
                top = jnp.max(scores, axis=0, keepdims=True)
                if not first:
                    top = jnp.maximum(top, tops[i])
                expo = jnp.exp(scores - top)
                total = jnp.sum(expo, axis=0, keepdims=True)
                weights = expo.astype(jnp.bfloat16)
                flipped = jnp.transpose(read(pl.ds(pl.multiple_of(width + col, LANES), LANES)))
                summed = jnp.concatenate(
                    [
                        jnp.dot(
                            flipped[:size], weights[:, :rows], preferred_element_type=jnp.float32
                        ),
                        jnp.dot(
                            flipped[size:], weights[:, rows:], preferred_element_type=jnp.float32
                        ),
                    ],
                    axis=1,
                )
                if not first:
                    factor = jnp.exp(tops[i] - top)
                    total = total + totals[i] * factor
                    summed = summed + acc[i] * factor
                done.append((i, top, total, summed))
            for i, top, total, summed in done:
                tops[i] = top
                totals[i] = total
                acc[i] = summed
            return carry

        lax.fori_loop(0, pairs // GROUP, body, 0)

    def landed(pieces):
        def read(cols):
            return jnp.concatenate(
                [kv[role - 1, part(h), cols] for role, h in pieces], axis=0
            )

        return read

    arrived(1, 0)
    arrived(1, 1)
    beside = landed([(1, 0), (1, 1)])
    attend(lambda cols: jnp.concatenate([fresh[:, cols], beside(cols)], axis=0), first=True)
    if chips == 4:
        plan = [((1, 0), (2, 1)), ((1, 1), (2, 0)), ((3, 0), (3, 1))]
    else:
        plan = [((j, 0), (j, 1)) for j in range(1, chips)]
    for pair in plan:
        for j, h in pair:
            relay(j, h)
        for j, h in pair:
            arrived(2 * j + 1, h)
        attend(landed([(2 * j + c, h) for j, h in pair for c in range(2)]))

    def finish(i, carry):
        result = acc[i] / totals[i]
        stacked = jnp.concatenate([result[:, :rows], result[:, rows:]], axis=0)
        cols = pl.ds(pl.multiple_of(i * LANES, LANES), LANES)
        normed[:, cols] = jnp.transpose(stacked).astype(jnp.bfloat16)
        return carry

    lax.fori_loop(0, pairs, finish, 0)
    loads[1].wait()

    def output(c, carry):
        cols = pl.ds(pl.multiple_of(c * CHUNK, CHUNK), CHUNK)
        proj = jnp.dot(normed[...], wo[:, cols], preferred_element_type=jnp.float32)
        gate = modulation[:, pl.ds(pl.multiple_of(2 * width + c * CHUNK, CHUNK), CHUNK)]
        layer_out[:, cols] = (mixed[:, cols] + gate * proj).astype(jnp.bfloat16)
        return carry

    lax.fori_loop(0, width // CHUNK, output, 0)

    for copy in edges + sent:
        copy.wait_send()


def remote(src, dst, send_sem, recv_sem, device):
    return pltpu.make_async_remote_copy(
        src_ref=src,
        dst_ref=dst,
        send_sem=send_sem,
        recv_sem=recv_sem,
        device_id={"patch": device},
        device_id_type=pl.DeviceIdType.MESH,
    )


def fold(state, scores, flipped, size, rows):
    top = jnp.max(scores, axis=0, keepdims=True)
    if state is not None:
        top = jnp.maximum(top, state[0])
    expo = jnp.exp(scores - top)
    total = jnp.sum(expo, axis=0, keepdims=True)
    weights = expo.astype(jnp.bfloat16)
    summed = jnp.concatenate(
        [
            jnp.dot(flipped[:size], weights[:, :rows], preferred_element_type=jnp.float32),
            jnp.dot(flipped[size:], weights[:, rows:], preferred_element_type=jnp.float32),
        ],
        axis=1,
    )
    if state is not None:
        factor = jnp.exp(state[0] - top)
        total = total + state[1] * factor
        summed = summed + state[2] * factor
    return top, total, summed


def pipeline(tasks, size, rows):
    states = {}
    waiting = None
    for task in tasks + [None]:
        ahead = None
        if task is not None:
            ahead = jnp.dot(task[1](), task[3], preferred_element_type=jnp.float32)
        if waiting is not None:
            (stream, _, values, _), scores = waiting
            states[stream] = fold(states.get(stream), scores, values(), size, rows)
        waiting = (task, ahead)
    return states


def blocked(flat, size, rows):
    zero = jnp.zeros((size, rows), flat.dtype)
    return jnp.concatenate(
        [
            jnp.concatenate([flat[:size], zero], axis=1),
            jnp.concatenate([zero, flat[size:]], axis=1),
        ],
        axis=0,
    )


def spread(
    count,
    timestep,
    action,
    latent,
    conv_weight,
    time_table,
    action_table,
    w_qkv,
    w_out,
    stale,
    layer_out,
    fresh,
    kv,
    wq,
    wo,
    halo,
    mixed,
    normed,
    flat,
    turned,
    asked,
    done,
    done_stats,
    back,
    back_stats,
    acc,
    tops,
    totals,
    modulation,
    halo_send,
    halo_recv,
    kv_send,
    kv_recv,
    relay_send,
    relay_recv,
    ask_send,
    ask_recv,
    back_send,
    back_recv,
    load_sem,
):
    rows, width = latent.shape
    size = width // HEADS
    pairs = width // LANES
    chips = count // 2
    share = width // chips
    mine = pairs // chips
    me = lax.axis_index("patch")
    core = me % 2
    chip = me // 2
    sibling = chip * 2 + (1 - core)

    def target(j):
        if chips == 4:
            return (chip, chip + 1 - 2 * (chip % 2), (chip + 2) % 4, 3 - chip)[j]
        return (chip + chips - j) % chips

    def source(j):
        if chips == 4:
            return target(j)
        return (chip + j) % chips

    loads = [
        pltpu.make_async_copy(w_qkv, wq, load_sem.at[0]),
        pltpu.make_async_copy(w_out, wo, load_sem.at[1]),
    ]
    for load in loads:
        load.start()

    barrier = pltpu.get_barrier_semaphore()
    for step in range(1, count):
        pl.semaphore_signal(
            barrier,
            inc=1,
            device_id={"patch": (me + step) % count},
            device_id_type=pl.DeviceIdType.MESH,
        )
    pl.semaphore_wait(barrier, count - 1)

    edges = []
    for slot, (start, device) in enumerate(
        ((rows - GRID_W, (me + 1) % count), (0, (me + count - 1) % count))
    ):
        copy = remote(
            latent.at[pl.ds(start, GRID_W)],
            halo.at[slot],
            halo_send.at[slot],
            halo_recv.at[slot],
            device,
        )
        copy.start()
        edges.append(copy)

    sent = []
    arriving = {}

    def piece(owner, side):
        start = pl.multiple_of(side * width + owner * share, LANES)
        return stale.at[:, pl.ds(start, share)]

    for j in range(chips):
        for side in range(2):
            copy = remote(
                piece(target(j), side),
                kv.at[2 * j if j else 1, :, pl.ds(side * share, share)],
                kv_send.at[j, side],
                kv_recv.at[j, side],
                target(j) * 2 + core if j else sibling,
            )
            copy.start()
            sent.append(copy)
            arriving[j, side] = copy
    for side in range(2):
        load = pltpu.make_async_copy(
            piece(chip, side), kv.at[0, :, pl.ds(side * share, share)], load_sem.at[2 + side]
        )
        load.start()
        loads.append(load)

    prepare(
        count, timestep, action, latent, conv_weight, time_table, action_table,
        halo, edges, mixed, normed, modulation,
    )

    loads[0].wait()
    per = CHUNK // LANES

    def project(c):
        cols = pl.ds(pl.multiple_of(c * CHUNK, CHUNK), CHUNK)
        return jnp.dot(normed[...], wq[:, cols], preferred_element_type=jnp.float32)

    def queries(c, carry):
        block = project(c) * size ** (-0.5)
        for u in range(per):
            flat[c * per + u] = jnp.transpose(block[:, u * LANES : (u + 1) * LANES]).astype(
                jnp.bfloat16
            )
        return carry

    lax.fori_loop(0, width // CHUNK, queries, 0)

    asking = {}
    for j in range(chips - 1, 0, -1):
        copy = remote(
            flat.at[pl.ds(target(j) * mine, mine)],
            asked.at[j - 1],
            ask_send.at[j - 1],
            ask_recv.at[j - 1],
            target(j) * 2 + core,
        )
        copy.start()
        sent.append(copy)
        asking[j] = copy

    def keys_values(c, carry):
        cols = pl.ds(pl.multiple_of(c * CHUNK, CHUNK), CHUNK)
        fresh[:, cols] = project(c + width // CHUNK).astype(jnp.bfloat16)
        return carry

    lax.fori_loop(0, 2 * width // CHUNK, keys_values, 0)

    def local(g, carry):
        def read(start):
            return fresh[:, pl.ds(pl.multiple_of(start, LANES), LANES)]

        def task(u):
            i = g * MANY + u
            return (
                u,
                lambda: read(i * LANES),
                lambda: jnp.transpose(read(width + i * LANES)),
                blocked(flat[i], size, rows),
            )

        found = pipeline([task(u) for u in range(MANY)], size, rows)
        for u in range(MANY):
            i = g * MANY + u
            tops[i], totals[i], acc[i] = found[u]
        return carry

    early = pairs // MANY - 1

    lax.fori_loop(0, early, local, 0)

    relays = {}

    def ready(chunk):
        for slot in chunk:
            j = slot // 2
            if slot == 0:
                loads[2].wait()
                loads[3].wait()
            elif slot == 1:
                arriving[0, 0].wait_recv()
                arriving[0, 1].wait_recv()
            elif slot % 2 == 0:
                arriving[j, 0].wait_recv()
                arriving[j, 1].wait_recv()
                relays[j] = remote(
                    kv.at[slot],
                    kv.at[slot + 1],
                    relay_send.at[j - 1],
                    relay_recv.at[j - 1],
                    sibling,
                )
                relays[j].start()
                sent.append(relays[j])
            else:
                relays[j].wait_recv()
        for slot in chunk:
            for i in range(mine):
                turned[i, :, pl.ds(slot * rows, rows)] = jnp.transpose(
                    kv[slot, :, pl.ds(share + i * LANES, LANES)]
                )

    def serve(j):
        slots = [slot for slot in range(count) if slot != 2 * j]
        chunks = [slots[n : n + 2] for n in range(0, count - 4, 2)] + [slots[count - 4 :]]
        if j == 0:
            near = [2 * n for n in range(1, chips - 1)]
            chunks = [[1] + near, [slot + 1 for slot in near], [count - 2], [count - 1]]
            chunks = [chunk for chunk in chunks if chunk]
        queries = [
            blocked(flat[chip * mine + i] if j == 0 else asked[j - 1, i], size, rows)
            for i in range(mine)
        ]

        def keys(chunk, i):
            def read():
                if j == 0 and i == 0:
                    ready(chunk)
                cols = pl.ds(i * LANES, LANES)
                return jnp.concatenate([kv[slot, :, cols] for slot in chunk], axis=0)

            return read

        def values(chunk, i):
            return lambda: jnp.concatenate(
                [turned[i, :, pl.ds(slot * rows, rows)] for slot in chunk], axis=1
            )

        tasks = [
            (i, keys(chunk, i), values(chunk, i), queries[i])
            for chunk in chunks
            for i in range(mine)
        ]
        for i, (top, total, summed) in pipeline(tasks, size, rows).items():
            result = (summed / total).astype(jnp.bfloat16)
            place, stats = (back.at[0], back_stats.at[0])
            if j > 0:
                place, stats = (done.at[j - 1], done_stats.at[j - 1])
            place[i] = result
            stats[i : i + 1, :] = top
            stats[mine + i : mine + i + 1, :] = total

    serve(0)
    ready([0])
    returning = []
    for j in range(chips - 1, 0, -1):
        asking[j].wait_recv()
        serve(j)
        for n, (src, dst) in enumerate(((done, back), (done_stats, back_stats))):
            copy = remote(
                src.at[j - 1],
                dst.at[j],
                back_send.at[j - 1, n],
                back_recv.at[j - 1, n],
                source(j) * 2 + core,
            )
            copy.start()
            sent.append(copy)
            returning.append(copy)

    lax.fori_loop(early, pairs // MANY, local, 0)

    def merge(j):
        def body(i, carry):
            g = target(j) * mine + i
            there = back_stats[j, pl.ds(i, 1), :]
            top = jnp.maximum(tops[g], there)
            one = jnp.exp(tops[g] - top)
            other = jnp.exp(there - top) * back_stats[j, pl.ds(mine + i, 1), :]
            total = totals[g] * one + other
            result = (acc[g] * one + back[j, i].astype(jnp.float32) * other) / total
            stacked = jnp.concatenate([result[:, :rows], result[:, rows:]], axis=0)
            cols = pl.ds(pl.multiple_of(g * LANES, LANES), LANES)
            normed[:, cols] = jnp.transpose(stacked).astype(jnp.bfloat16)
            return carry

        lax.fori_loop(0, mine, body, 0)

    merge(0)
    for j in range(chips - 1, 0, -1):
        for copy in returning[2 * (chips - 1 - j) : 2 * (chips - j)]:
            copy.wait_recv()
        merge(j)
    loads[1].wait()

    def output(c, carry):
        cols = pl.ds(pl.multiple_of(c * CHUNK, CHUNK), CHUNK)
        proj = jnp.dot(normed[...], wo[:, cols], preferred_element_type=jnp.float32)
        gate = modulation[:, pl.ds(pl.multiple_of(2 * width + c * CHUNK, CHUNK), CHUNK)]
        layer_out[:, cols] = (mixed[:, cols] + gate * proj).astype(jnp.bfloat16)
        return carry

    lax.fori_loop(0, width // CHUNK, output, 0)

    for copy in edges + sent:
        copy.wait_send()


def per_device(
    count, latent, conv_weight, time_table, action_table, timestep, action, w_qkv, w_out, stale_kv
):
    rows, width = latent.shape
    pairs = width // LANES
    size = width // HEADS
    chips = count // 2
    vmem = pl.BlockSpec(memory_space=pltpu.VMEM)
    smem = pl.BlockSpec(memory_space=pltpu.SMEM)
    anywhere = pl.BlockSpec(memory_space=pl.ANY)
    dma = pltpu.SemaphoreType.DMA
    front = [
        pltpu.VMEM(w_qkv.shape, jnp.bfloat16),
        pltpu.VMEM(w_out.shape, jnp.bfloat16),
        pltpu.VMEM((2, GRID_W, width), jnp.bfloat16),
        pltpu.VMEM((rows, width), jnp.float32),
        pltpu.VMEM((rows, width), jnp.bfloat16),
    ]
    state = [
        pltpu.VMEM((pairs, size, 2 * rows), jnp.float32),
        pltpu.VMEM((pairs, 1, 2 * rows), jnp.float32),
        pltpu.VMEM((pairs, 1, 2 * rows), jnp.float32),
        pltpu.VMEM((1, 3 * width), jnp.float32),
        dma((2,)),
        dma((2,)),
        dma((chips, 2)),
    ]
    if pairs % chips == 0 and width % (chips * LANES) == 0:
        body = spread
        mine = pairs // chips
        lines = 8 * pl.cdiv(2 * mine, 8)
        scratch = [
            pltpu.VMEM((count, rows, 2 * width // chips), jnp.bfloat16),
            *front,
            pltpu.VMEM((pairs, LANES, rows), jnp.bfloat16),
            pltpu.VMEM((mine, LANES, count * rows), jnp.bfloat16),
            pltpu.VMEM((chips - 1, mine, LANES, rows), jnp.bfloat16),
            pltpu.VMEM((chips - 1, mine, size, 2 * rows), jnp.bfloat16),
            pltpu.VMEM((chips - 1, lines, 2 * rows), jnp.float32),
            pltpu.VMEM((chips, mine, size, 2 * rows), jnp.bfloat16),
            pltpu.VMEM((chips, lines, 2 * rows), jnp.float32),
            *state,
            dma((chips, 2)),
            dma((chips - 1,)),
            dma((chips - 1,)),
            dma((chips - 1,)),
            dma((chips - 1,)),
            dma((chips - 1, 2)),
            dma((chips - 1, 2)),
            dma((4,)),
        ]
    else:
        body = kernel
        scratch = [
            pltpu.VMEM((count - 1, rows, 2 * width), jnp.bfloat16),
            *front,
            pltpu.VMEM((pairs, LANES, 2 * rows), jnp.bfloat16),
            *state,
            dma((chips - 1, 2)),
            dma((2,)),
            dma((count - 1, 2)),
            dma((2,)),
        ]
    return pl.pallas_call(
        functools.partial(body, count),
        out_shape=(
            jax.ShapeDtypeStruct((rows, width), jnp.bfloat16),
            jax.ShapeDtypeStruct((rows, 2 * width), jnp.bfloat16),
        ),
        in_specs=[smem, smem, vmem, vmem, vmem, vmem, anywhere, anywhere, anywhere],
        out_specs=(vmem, vmem),
        scratch_shapes=scratch,
        compiler_params=pltpu.CompilerParams(
            collective_id=0, has_side_effects=True, vmem_limit_bytes=60 * 2**20
        ),
        cost_estimate=pl.CostEstimate(
            flops=8 * 10**9, bytes_accessed=30 * 2**20, transcendentals=13 * 10**6
        ),
    )(timestep, action, latent, conv_weight, time_table, action_table, w_qkv, w_out, stale_kv)


def solution(mesh):
    in_specs = (
        P(("frame", "patch"), None),
        P(),
        P(),
        P(),
        P("frame"),
        P("frame"),
        P(),
        P(),
        P(("frame", "patch"), None),
    )
    out_specs = (P(("frame", "patch"), None), P(("frame", "patch"), None))
    return jax.shard_map(
        functools.partial(per_device, mesh.shape["patch"]),
        mesh=mesh,
        in_specs=in_specs,
        out_specs=out_specs,
        check_vma=False,
    )
```

```python
import functools

import jax
import jax.numpy as jnp
from jax import lax
from jax.experimental import pallas as pl
from jax.experimental.pallas import tpu as pltpu
from jax.sharding import PartitionSpec as P

HEADS = 24
GRID_W = 64
LANES = 128
GROUP = 2
MANY = 4
CHUNK = 512


def prepare(
    count,
    timestep,
    action,
    latent,
    conv_weight,
    time_table,
    action_table,
    halo,
    edges,
    mixed,
    normed,
    modulation,
):
    rows, width = latent.shape
    me = lax.axis_index("patch")

    def pick(table, index):
        hot = lax.broadcasted_iota(jnp.int32, table.shape, 0) == index
        return jnp.sum(
            jnp.where(hot, table[...].astype(jnp.float32), 0.0), axis=0, keepdims=True
        )

    modulation[...] = pick(time_table, timestep[0]) + pick(action_table, action[0])

    nrows = rows // GRID_W

    def stem(r):
        def body(c, carry):
            cols = pl.ds(pl.multiple_of(c * 2 * LANES, 2 * LANES), 2 * LANES)
            taps = conv_weight[:, cols]
            lines = []
            for a in (r - 1, r, r + 1):
                if a < 0:
                    line = jnp.where(me > 0, halo[0, :, cols].astype(jnp.float32), 0.0)
                elif a >= nrows:
                    line = jnp.where(me < count - 1, halo[1, :, cols].astype(jnp.float32), 0.0)
                else:
                    line = latent[pl.ds(a * GRID_W, GRID_W), cols].astype(jnp.float32)
                lines.append(line)
            sums = []
            for b in range(3):
                total = lines[0] * taps[b : b + 1]
                total = total + lines[1] * taps[3 + b : 4 + b]
                sums.append(total + lines[2] * taps[6 + b : 7 + b])
            place = lax.broadcasted_iota(jnp.int32, sums[0].shape, 0)
            before = jnp.where(place == 0, 0.0, pltpu.roll(sums[0], 1, 0))
            after = jnp.where(place == GRID_W - 1, 0.0, pltpu.roll(sums[2], GRID_W - 1, 0))
            mixed[pl.ds(r * GRID_W, GRID_W), cols] = lines[1] + sums[1] + (before + after)
            return carry

        lax.fori_loop(0, width // (2 * LANES), body, 0)

    for r in range(1, nrows - 1):
        stem(r)
    for edge in edges:
        edge.wait_recv()
    stem(0)
    stem(nrows - 1)

    def norm(r, carry):
        span = pl.ds(pl.multiple_of(r * 32, 32), 32)
        x = mixed[span, :]
        mean = jnp.mean(x, axis=1, keepdims=True)
        centred = x - mean
        var = jnp.mean(centred * centred, axis=1, keepdims=True)
        gain = 1.0 + modulation[:, width : 2 * width]
        normed[span, :] = (
            centred * lax.rsqrt(var + 1e-06) * gain + modulation[:, :width]
        ).astype(jnp.bfloat16)
        return carry

    lax.fori_loop(0, rows // 32, norm, 0)


def kernel(
    count,
    timestep,
    action,
    latent,
    conv_weight,
    time_table,
    action_table,
    w_qkv,
    w_out,
    stale,
    layer_out,
    fresh,
    kv,
    wq,
    wo,
    halo,
    mixed,
    normed,
    qbd,
    acc,
    tops,
    totals,
    modulation,
    halo_send,
    halo_recv,
    own_send,
    relay_send,
    cross_send,
    recv,
    load_sem,
):
    rows, width = latent.shape
    half = rows // 2
    size = width // HEADS
    pairs = width // LANES
    chips = count // 2
    me = lax.axis_index("patch")
    core = me % 2
    chip = me // 2
    sibling = chip * 2 + (1 - core)

    def part(h):
        return pl.ds(h * half, half)

    def target(j):
        if chips == 4:
            other = chip + 1 - 2 * (chip % 2) if j == 1 else (chip + 2) % 4
        else:
            other = (chip + chips - j) % chips
        return other * 2 + core

    def send(src, role, h, sem, device):
        copy = pltpu.make_async_remote_copy(
            src_ref=src,
            dst_ref=kv.at[role - 1, part(h)],
            send_sem=sem,
            recv_sem=recv.at[role - 1, h],
            device_id={"patch": device},
            device_id_type=pl.DeviceIdType.MESH,
        )
        copy.start()
        return copy

    def arrived(role, h):
        pltpu.make_async_remote_copy(
            src_ref=kv.at[role - 1, part(h)],
            dst_ref=kv.at[role - 1, part(h)],
            send_sem=cross_send.at[0],
            recv_sem=recv.at[role - 1, h],
            device_id={"patch": sibling},
            device_id_type=pl.DeviceIdType.MESH,
        ).wait_recv()

    loads = [
        pltpu.make_async_copy(w_qkv, wq, load_sem.at[0]),
        pltpu.make_async_copy(w_out, wo, load_sem.at[1]),
    ]
    for load in loads:
        load.start()

    barrier = pltpu.get_barrier_semaphore()
    for step in range(1, count):
        pl.semaphore_signal(
            barrier,
            inc=1,
            device_id={"patch": (me + step) % count},
            device_id_type=pl.DeviceIdType.MESH,
        )
    pl.semaphore_wait(barrier, count - 1)

    edges = []
    for slot, (start, device) in enumerate(
        ((rows - GRID_W, (me + 1) % count), (0, (me + count - 1) % count))
    ):
        copy = pltpu.make_async_remote_copy(
            src_ref=latent.at[pl.ds(start, GRID_W)],
            dst_ref=halo.at[slot],
            send_sem=halo_send.at[slot],
            recv_sem=halo_recv.at[slot],
            device_id={"patch": device},
            device_id_type=pl.DeviceIdType.MESH,
        )
        copy.start()
        edges.append(copy)

    sent = []
    direct = (1, 2) if chips == 4 else tuple(range(1, chips))
    for order in range(2):
        for j in direct:
            h = order if j % 2 == 1 else 1 - order
            sent.append(send(stale.at[part(h)], 2 * j, h, own_send.at[j, h], target(j)))
        sent.append(send(stale.at[part(order)], 1, order, own_send.at[0, order], sibling))

    def relay(j, h):
        arrived(2 * j, h)
        if chips == 4 and (j, h) == (1, 0):
            sent.append(send(kv.at[1, part(0)], 6, 0, cross_send.at[0], target(2)))
        if chips == 4 and (j, h) == (2, 1):
            sent.append(send(kv.at[3, part(1)], 6, 1, cross_send.at[1], target(1)))
        sent.append(
            send(kv.at[2 * j - 1, part(h)], 2 * j + 1, h, relay_send.at[j - 1, h], sibling)
        )

    prepare(
        count, timestep, action, latent, conv_weight, time_table, action_table,
        halo, edges, mixed, normed, modulation,
    )

    loads[0].wait()
    qbd[...] = jnp.zeros_like(qbd)
    per = CHUNK // LANES

    def project(c):
        cols = pl.ds(pl.multiple_of(c * CHUNK, CHUNK), CHUNK)
        return jnp.dot(normed[...], wq[:, cols], preferred_element_type=jnp.float32)

    def queries(c, carry):
        block = project(c) * size ** (-0.5)
        for u in range(per):
            flipped = jnp.transpose(block[:, u * LANES : (u + 1) * LANES]).astype(jnp.bfloat16)
            qbd[c * per + u, :size, :rows] = flipped[:size]
            qbd[c * per + u, size:, rows:] = flipped[size:]
        return carry

    lax.fori_loop(0, width // CHUNK, queries, 0)

    def keys_values(c, carry):
        cols = pl.ds(pl.multiple_of(c * CHUNK, CHUNK), CHUNK)
        fresh[:, cols] = project(c + width // CHUNK).astype(jnp.bfloat16)
        return carry

    lax.fori_loop(0, 2 * width // CHUNK, keys_values, 0)

    def attend(read, first=False):
        def body(g, carry):
            done = []
            for u in range(GROUP):
                i = g * GROUP + u
                col = pl.multiple_of(i * LANES, LANES)
                scores = jnp.dot(
                    read(pl.ds(col, LANES)), qbd[i], preferred_element_type=jnp.float32
                )
                top = jnp.max(scores, axis=0, keepdims=True)
                if not first:
                    top = jnp.maximum(top, tops[i])
                expo = jnp.exp(scores - top)
                total = jnp.sum(expo, axis=0, keepdims=True)
                weights = expo.astype(jnp.bfloat16)
                flipped = jnp.transpose(read(pl.ds(pl.multiple_of(width + col, LANES), LANES)))
                summed = jnp.concatenate(
                    [
                        jnp.dot(
                            flipped[:size], weights[:, :rows], preferred_element_type=jnp.float32
                        ),
                        jnp.dot(
                            flipped[size:], weights[:, rows:], preferred_element_type=jnp.float32
                        ),
                    ],
                    axis=1,
                )
                if not first:
                    factor = jnp.exp(tops[i] - top)
                    total = total + totals[i] * factor
                    summed = summed + acc[i] * factor
                done.append((i, top, total, summed))
            for i, top, total, summed in done:
                tops[i] = top
                totals[i] = total
                acc[i] = summed
            return carry

        lax.fori_loop(0, pairs // GROUP, body, 0)

    def landed(pieces):
        def read(cols):
            return jnp.concatenate(
                [kv[role - 1, part(h), cols] for role, h in pieces], axis=0
            )

        return read

    arrived(1, 0)
    arrived(1, 1)
    beside = landed([(1, 0), (1, 1)])
    attend(lambda cols: jnp.concatenate([fresh[:, cols], beside(cols)], axis=0), first=True)
    if chips == 4:
        plan = [((1, 0), (2, 1)), ((1, 1), (2, 0)), ((3, 0), (3, 1))]
    else:
        plan = [((j, 0), (j, 1)) for j in range(1, chips)]
    for pair in plan:
        for j, h in pair:
            relay(j, h)
        for j, h in pair:
            arrived(2 * j + 1, h)
        attend(landed([(2 * j + c, h) for j, h in pair for c in range(2)]))

    def finish(i, carry):
        result = acc[i] / totals[i]
        stacked = jnp.concatenate([result[:, :rows], result[:, rows:]], axis=0)
        cols = pl.ds(pl.multiple_of(i * LANES, LANES), LANES)
        normed[:, cols] = jnp.transpose(stacked).astype(jnp.bfloat16)
        return carry

    lax.fori_loop(0, pairs, finish, 0)
    loads[1].wait()

    def output(c, carry):
        cols = pl.ds(pl.multiple_of(c * CHUNK, CHUNK), CHUNK)
        proj = jnp.dot(normed[...], wo[:, cols], preferred_element_type=jnp.float32)
        gate = modulation[:, pl.ds(pl.multiple_of(2 * width + c * CHUNK, CHUNK), CHUNK)]
        layer_out[:, cols] = (mixed[:, cols] + gate * proj).astype(jnp.bfloat16)
        return carry

    lax.fori_loop(0, width // CHUNK, output, 0)

    for copy in edges + sent:
        copy.wait_send()


def remote(src, dst, send_sem, recv_sem, device):
    return pltpu.make_async_remote_copy(
        src_ref=src,
        dst_ref=dst,
        send_sem=send_sem,
        recv_sem=recv_sem,
        device_id={"patch": device},
        device_id_type=pl.DeviceIdType.MESH,
    )


def fold(state, scores, flipped, size, rows):
    top = jnp.max(scores, axis=0, keepdims=True)
    if state is not None:
        top = jnp.maximum(top, state[0])
    expo = jnp.exp(scores - top)
    total = jnp.sum(expo, axis=0, keepdims=True)
    weights = expo.astype(jnp.bfloat16)
    summed = jnp.concatenate(
        [
            jnp.dot(flipped[:size], weights[:, :rows], preferred_element_type=jnp.float32),
            jnp.dot(flipped[size:], weights[:, rows:], preferred_element_type=jnp.float32),
        ],
        axis=1,
    )
    if state is not None:
        factor = jnp.exp(state[0] - top)
        total = total + state[1] * factor
        summed = summed + state[2] * factor
    return top, total, summed


def pipeline(tasks, size, rows, finish):
    states = {}
    last = {task[0]: n for n, task in enumerate(tasks)}
    waiting = None
    for n, task in enumerate(tasks + [None]):
        ahead = None
        if task is not None:
            ahead = jnp.dot(task[1](), task[3], preferred_element_type=jnp.float32)
        if waiting is not None:
            (stream, _, values, _), scores = waiting
            states[stream] = fold(states.get(stream), scores, values(), size, rows)
            if last[stream] == n - 1:
                finish(stream, states[stream])
        waiting = (task, ahead)


def blocked(flat, size, rows):
    zero = jnp.zeros((size, rows), flat.dtype)
    return jnp.concatenate(
        [
            jnp.concatenate([flat[:size], zero], axis=1),
            jnp.concatenate([zero, flat[size:]], axis=1),
        ],
        axis=0,
    )


def spread(
    count,
    timestep,
    action,
    latent,
    conv_weight,
    time_table,
    action_table,
    w_qkv,
    w_out,
    stale,
    layer_out,
    fresh,
    kv,
    wq,
    wo,
    halo,
    mixed,
    normed,
    flat,
    turned,
    asked,
    done,
    done_stats,
    back,
    back_stats,
    acc,
    tops,
    totals,
    modulation,
    halo_send,
    halo_recv,
    kv_send,
    kv_recv,
    relay_send,
    relay_recv,
    ask_send,
    ask_recv,
    back_send,
    back_recv,
    load_sem,
):
    rows, width = latent.shape
    size = width // HEADS
    pairs = width // LANES
    chips = count // 2
    share = width // chips
    mine = pairs // chips
    me = lax.axis_index("patch")
    core = me % 2
    chip = me // 2
    sibling = chip * 2 + (1 - core)

    def target(j):
        if chips == 4:
            return (chip, chip + 1 - 2 * (chip % 2), (chip + 2) % 4, 3 - chip)[j]
        return (chip + chips - j) % chips

    def source(j):
        if chips == 4:
            return target(j)
        return (chip + j) % chips

    loads = [
        pltpu.make_async_copy(w_qkv, wq, load_sem.at[0]),
        pltpu.make_async_copy(w_out, wo, load_sem.at[1]),
    ]
    for load in loads:
        load.start()

    barrier = pltpu.get_barrier_semaphore()
    for step in range(1, count):
        pl.semaphore_signal(
            barrier,
            inc=1,
            device_id={"patch": (me + step) % count},
            device_id_type=pl.DeviceIdType.MESH,
        )
    pl.semaphore_wait(barrier, count - 1)

    edges = []
    for slot, (start, device) in enumerate(
        ((rows - GRID_W, (me + 1) % count), (0, (me + count - 1) % count))
    ):
        copy = remote(
            latent.at[pl.ds(start, GRID_W)],
            halo.at[slot],
            halo_send.at[slot],
            halo_recv.at[slot],
            device,
        )
        copy.start()
        edges.append(copy)

    sent = []
    arriving = {}

    def piece(owner, side):
        start = pl.multiple_of(side * width + owner * share, LANES)
        return stale.at[:, pl.ds(start, share)]

    for j in range(chips):
        for side in range(2):
            copy = remote(
                piece(target(j), side),
                kv.at[2 * j if j else 1, :, pl.ds(side * share, share)],
                kv_send.at[j, side],
                kv_recv.at[j, side],
                target(j) * 2 + core if j else sibling,
            )
            copy.start()
            sent.append(copy)
            arriving[j, side] = copy
    for side in range(2):
        load = pltpu.make_async_copy(
            piece(chip, side), kv.at[0, :, pl.ds(side * share, share)], load_sem.at[2 + side]
        )
        load.start()
        loads.append(load)

    prepare(
        count, timestep, action, latent, conv_weight, time_table, action_table,
        halo, edges, mixed, normed, modulation,
    )

    loads[0].wait()
    per = CHUNK // LANES

    def project(c):
        cols = pl.ds(pl.multiple_of(c * CHUNK, CHUNK), CHUNK)
        return jnp.dot(normed[...], wq[:, cols], preferred_element_type=jnp.float32)

    def queries(c, carry):
        block = project(c) * size ** (-0.5)
        for u in range(per):
            flat[c * per + u] = jnp.transpose(block[:, u * LANES : (u + 1) * LANES]).astype(
                jnp.bfloat16
            )
        return carry

    lax.fori_loop(0, width // CHUNK, queries, 0)

    asking = {}
    for j in range(chips - 1, 0, -1):
        copy = remote(
            flat.at[pl.ds(target(j) * mine, mine)],
            asked.at[j - 1],
            ask_send.at[j - 1],
            ask_recv.at[j - 1],
            target(j) * 2 + core,
        )
        copy.start()
        sent.append(copy)
        asking[j] = copy

    def keys_values(c, carry):
        cols = pl.ds(pl.multiple_of(c * CHUNK, CHUNK), CHUNK)
        fresh[:, cols] = project(c + width // CHUNK).astype(jnp.bfloat16)
        return carry

    lax.fori_loop(0, 2 * width // CHUNK, keys_values, 0)

    def local(g, carry):
        def read(start):
            return fresh[:, pl.ds(pl.multiple_of(start, LANES), LANES)]

        def task(u):
            i = g * MANY + u
            return (
                u,
                lambda: read(i * LANES),
                lambda: jnp.transpose(read(width + i * LANES)),
                blocked(flat[i], size, rows),
            )

        def finish(u, state):
            i = g * MANY + u
            tops[i], totals[i], acc[i] = state

        pipeline([task(u) for u in range(MANY)], size, rows, finish)
        return carry

    early = pairs // MANY - 1

    lax.fori_loop(0, early, local, 0)

    relays = {}

    def ready(chunk):
        for slot in chunk:
            j = slot // 2
            if slot == 0:
                loads[2].wait()
                loads[3].wait()
            elif slot == 1:
                arriving[0, 0].wait_recv()
                arriving[0, 1].wait_recv()
            elif slot % 2 == 0:
                arriving[j, 0].wait_recv()
                arriving[j, 1].wait_recv()
                relays[j] = remote(
                    kv.at[slot],
                    kv.at[slot + 1],
                    relay_send.at[j - 1],
                    relay_recv.at[j - 1],
                    sibling,
                )
                relays[j].start()
                sent.append(relays[j])
            else:
                relays[j].wait_recv()
        for slot in chunk:
            for i in range(mine):
                turned[i, :, pl.ds(slot * rows, rows)] = jnp.transpose(
                    kv[slot, :, pl.ds(share + i * LANES, LANES)]
                )

    def serve(j):
        slots = [slot for slot in range(count) if slot != 2 * j]
        chunks = [slots[n : n + 2] for n in range(0, count - 4, 2)] + [slots[count - 4 :]]
        if j == 0:
            near = [2 * n for n in range(1, chips - 1)]
            chunks = [[1] + near, [slot + 1 for slot in near], [count - 2], [count - 1]]
            chunks = [chunk for chunk in chunks if chunk]
        queries = [
            blocked(flat[chip * mine + i] if j == 0 else asked[j - 1, i], size, rows)
            for i in range(mine)
        ]

        def keys(chunk, i):
            def read():
                if j == 0 and i == 0:
                    ready(chunk)
                cols = pl.ds(i * LANES, LANES)
                return jnp.concatenate([kv[slot, :, cols] for slot in chunk], axis=0)

            return read

        def values(chunk, i):
            return lambda: jnp.concatenate(
                [turned[i, :, pl.ds(slot * rows, rows)] for slot in chunk], axis=1
            )

        order = [(i, chunk) for chunk in chunks for i in range(mine)]
        if j == 1:
            order = [(i, chunk) for i in range(mine) for chunk in chunks]
        tasks = [(i, keys(chunk, i), values(chunk, i), queries[i]) for i, chunk in order]

        def leave(src, dst, n):
            copy = remote(
                src, dst, back_send.at[j - 1, n], back_recv.at[j - 1, n], source(j) * 2 + core
            )
            copy.start()
            sent.append(copy)
            returning.setdefault(j, []).append(copy)

        def finish(i, state):
            top, total, summed = state
            place, stats = (back.at[0], back_stats.at[0])
            if j > 0:
                place, stats = (done.at[j - 1], done_stats.at[j - 1])
            place[i] = (summed / total).astype(jnp.bfloat16)
            stats[i : i + 1, :] = top
            stats[mine + i : mine + i + 1, :] = total
            if j > 0:
                leave(done.at[j - 1, i], back.at[j, i], i)

        pipeline(tasks, size, rows, finish)
        if j > 0:
            leave(done_stats.at[j - 1], back_stats.at[j], mine)

    returning = {}
    serve(0)
    ready([0])
    for j in range(chips - 1, 0, -1):
        asking[j].wait_recv()
        serve(j)

    lax.fori_loop(early, pairs // MANY, local, 0)

    def merge(j):
        def body(i, carry):
            g = target(j) * mine + i
            there = back_stats[j, pl.ds(i, 1), :]
            top = jnp.maximum(tops[g], there)
            one = jnp.exp(tops[g] - top)
            other = jnp.exp(there - top) * back_stats[j, pl.ds(mine + i, 1), :]
            total = totals[g] * one + other
            result = (acc[g] * one + back[j, i].astype(jnp.float32) * other) / total
            stacked = jnp.concatenate([result[:, :rows], result[:, rows:]], axis=0)
            cols = pl.ds(pl.multiple_of(g * LANES, LANES), LANES)
            normed[:, cols] = jnp.transpose(stacked).astype(jnp.bfloat16)
            return carry

        lax.fori_loop(0, mine, body, 0)

    merge(0)
    for j in range(chips - 1, 0, -1):
        for copy in returning[j]:
            copy.wait_recv()
        merge(j)
    loads[1].wait()

    def output(c, carry):
        cols = pl.ds(pl.multiple_of(c * CHUNK, CHUNK), CHUNK)
        proj = jnp.dot(normed[...], wo[:, cols], preferred_element_type=jnp.float32)
        gate = modulation[:, pl.ds(pl.multiple_of(2 * width + c * CHUNK, CHUNK), CHUNK)]
        layer_out[:, cols] = (mixed[:, cols] + gate * proj).astype(jnp.bfloat16)
        return carry

    lax.fori_loop(0, width // CHUNK, output, 0)

    for copy in edges + sent:
        copy.wait_send()


def per_device(
    count, latent, conv_weight, time_table, action_table, timestep, action, w_qkv, w_out, stale_kv
):
    rows, width = latent.shape
    pairs = width // LANES
    size = width // HEADS
    chips = count // 2
    vmem = pl.BlockSpec(memory_space=pltpu.VMEM)
    smem = pl.BlockSpec(memory_space=pltpu.SMEM)
    anywhere = pl.BlockSpec(memory_space=pl.ANY)
    dma = pltpu.SemaphoreType.DMA
    front = [
        pltpu.VMEM(w_qkv.shape, jnp.bfloat16),
        pltpu.VMEM(w_out.shape, jnp.bfloat16),
        pltpu.VMEM((2, GRID_W, width), jnp.bfloat16),
        pltpu.VMEM((rows, width), jnp.float32),
        pltpu.VMEM((rows, width), jnp.bfloat16),
    ]
    state = [
        pltpu.VMEM((pairs, size, 2 * rows), jnp.float32),
        pltpu.VMEM((pairs, 1, 2 * rows), jnp.float32),
        pltpu.VMEM((pairs, 1, 2 * rows), jnp.float32),
        pltpu.VMEM((1, 3 * width), jnp.float32),
        dma((2,)),
        dma((2,)),
        dma((chips, 2)),
    ]
    if pairs % chips == 0 and width % (chips * LANES) == 0:
        body = spread
        mine = pairs // chips
        lines = 8 * pl.cdiv(2 * mine, 8)
        scratch = [
            pltpu.VMEM((count, rows, 2 * width // chips), jnp.bfloat16),
            *front,
            pltpu.VMEM((pairs, LANES, rows), jnp.bfloat16),
            pltpu.VMEM((mine, LANES, count * rows), jnp.bfloat16),
            pltpu.VMEM((chips - 1, mine, LANES, rows), jnp.bfloat16),
            pltpu.VMEM((chips - 1, mine, size, 2 * rows), jnp.bfloat16),
            pltpu.VMEM((chips - 1, lines, 2 * rows), jnp.float32),
            pltpu.VMEM((chips, mine, size, 2 * rows), jnp.bfloat16),
            pltpu.VMEM((chips, lines, 2 * rows), jnp.float32),
            *state,
            dma((chips, 2)),
            dma((chips - 1,)),
            dma((chips - 1,)),
            dma((chips - 1,)),
            dma((chips - 1,)),
            dma((chips - 1, mine + 1)),
            dma((chips - 1, mine + 1)),
            dma((4,)),
        ]
    else:
        body = kernel
        scratch = [
            pltpu.VMEM((count - 1, rows, 2 * width), jnp.bfloat16),
            *front,
            pltpu.VMEM((pairs, LANES, 2 * rows), jnp.bfloat16),
            *state,
            dma((chips - 1, 2)),
            dma((2,)),
            dma((count - 1, 2)),
            dma((2,)),
        ]
    return pl.pallas_call(
        functools.partial(body, count),
        out_shape=(
            jax.ShapeDtypeStruct((rows, width), jnp.bfloat16),
            jax.ShapeDtypeStruct((rows, 2 * width), jnp.bfloat16),
        ),
        in_specs=[smem, smem, vmem, vmem, vmem, vmem, anywhere, anywhere, anywhere],
        out_specs=(vmem, vmem),
        scratch_shapes=scratch,
        compiler_params=pltpu.CompilerParams(
            collective_id=0, has_side_effects=True, vmem_limit_bytes=60 * 2**20
        ),
        cost_estimate=pl.CostEstimate(
            flops=8 * 10**9, bytes_accessed=30 * 2**20, transcendentals=13 * 10**6
        ),
    )(timestep, action, latent, conv_weight, time_table, action_table, w_qkv, w_out, stale_kv)


def solution(mesh):
    in_specs = (
        P(("frame", "patch"), None),
        P(),
        P(),
        P(),
        P("frame"),
        P("frame"),
        P(),
        P(),
        P(("frame", "patch"), None),
    )
    out_specs = (P(("frame", "patch"), None), P(("frame", "patch"), None))
    return jax.shard_map(
        functools.partial(per_device, mesh.shape["patch"]),
        mesh=mesh,
        in_specs=in_specs,
        out_specs=out_specs,
        check_vma=False,
    )
```
